128 devices in a mesh: seq: 32 (over x_lo, z, y), tp: 4 (over x_hi, core).
Axes of the slice: x: 4 (x_hi: 2, x_lo: 2; x = x_hi * 2 + x_lo), y: 4, z: 4, core: 2. Of those that a mesh axis runs over, the one named last changes fastest.
Arguments:
- inputs: bfloat16 [24576, 768], P('seq'), may hold values from -6 to 6
- cotangent: bfloat16 [24576, 768], P('seq'), may hold values from -6 to 6
- lengths: int32 [7], replicated, may hold values from 1 to 4096, 24576 in all
- query_codes: int32 [24576, 32], P('seq'), may hold values from 0 to 255
- key_codes: int32 [24576, 32], P('seq'), may hold values from 0 to 255
- masked: int32 [24576], P('seq'), may hold values from 0 to 1, as said below
- entry_weight: float32 [768, 3, 768], P('seq', None, 'tp'), may hold values from -0.21875 to 0.21875
- entry_moment: float32 [768, 3, 768], P('seq', None, 'tp'), may hold values from -448 to 448
- entry_square: float32 [768, 3, 768], P('seq', None, 'tp'), may hold values from 6144 to 24576
- merge_weight: float32 [768, 768], P('tp', 'seq'), may hold values from -0.21875 to 0.21875
- merge_moment: float32 [768, 768], P('tp', 'seq'), may hold values from -1024 to 1024
- merge_square: float32 [768, 768], P('tp', 'seq'), may hold values from 36864 to 147456
- expand_weight: float32 [768, 3072], P('seq', 'tp'), may hold values from -0.21875 to 0.21875
- expand_moment: float32 [768, 3072], P('seq', 'tp'), may hold values from -256 to 256
- expand_square: float32 [768, 3072], P('seq', 'tp'), may hold values from 2457.6 to 9830.4
- reduce_weight: float32 [3072, 768], P('tp', 'seq'), may hold values from -0.109375 to 0.109375
- reduce_moment: float32 [3072, 768], P('tp', 'seq'), may hold values from -640 to 640
- reduce_square: float32 [3072, 768], P('tp', 'seq'), may hold values from 9830.4 to 39321.6
- split_bias: float32 [12, 448], P('tp', 'seq'), may hold values from -3 to 3
- split_moment: float32 [12, 448], P('tp', 'seq'), may hold values from -384 to 384
- split_square: float32 [12, 448], P('tp', 'seq'), may hold values from 2457.6 to 9830.4
- width_params: float32 [6, 768], P(None, 'seq'), may hold values from -0.9 to 1.15, as said below
- width_moment: float32 [6, 768], P(None, 'seq'), may hold values from -896 to 896
- width_square: float32 [6, 768], P(None, 'seq'), may hold values from 24576 to 98304
Outputs:
- layer_out: bfloat16 [24576, 768], P('seq')
- input_grad: float32 [24576, 768], P('seq')
- entry_updated: float32 [768, 3, 768], P('seq', None, 'tp')
- entry_momentum: float32 [768, 3, 768], P('seq', None, 'tp')
- entry_squares: float32 [768, 3, 768], P('seq', None, 'tp')
- merge_updated: float32 [768, 768], P('tp', 'seq')
- merge_momentum: float32 [768, 768], P('tp', 'seq')
- merge_squares: float32 [768, 768], P('tp', 'seq')
- expand_updated: float32 [768, 3072], P('seq', 'tp')
- expand_momentum: float32 [768, 3072], P('seq', 'tp')
- expand_squares: float32 [768, 3072], P('seq', 'tp')
- reduce_updated: float32 [3072, 768], P('tp', 'seq')
- reduce_momentum: float32 [3072, 768], P('tp', 'seq')
- reduce_squares: float32 [3072, 768], P('tp', 'seq')
- split_updated: float32 [12, 448], P('tp', 'seq')
- split_momentum: float32 [12, 448], P('tp', 'seq')
- split_squares: float32 [12, 448], P('tp', 'seq')
- width_updated: float32 [6, 768], P(None, 'seq')
- width_momentum: float32 [6, 768], P(None, 'seq')
- width_squares: float32 [6, 768], P(None, 'seq')
The draws below stay inside these ranges and needn't reach their ends.
Inputs may be any that keep to these rules, and one draw needn't show every extreme that they name: The lengths sum to 24576; the longest is 4096. `masked`: 1 marks a position whose output carries a gradient. `width_params`: rows 2 and 4 are gains, the others biases.
All inputs are finite; a program needn't handle non-finite values.
Results may differ from the reference program's by a relative error of at most 0.01.
Values may be sent and summed in bfloat16 or wider, within the bound.
No kernel may reach another device: no remote copies, remote signals or barrier semaphores. Data moves between devices by JAX's collectives and lax.ppermute only.
A program may use at most 448 MiB of HBM per device.

```python
import math
import jax
import jax.numpy as jnp
import numpy as np
from jax import lax

D = 768
H = 12
DH = 64
FF = 3072
HASHES = 32
BUCKETS = 256
TAU = 8
STEP = 10
LENGTH = 4096
TOKENS = 24576
SEQS = 7
N_SEQ = 32


def draw_masked(key, part):
    key = jax.random.fold_in(key, 7)
    rolls = jax.random.randint(key, (TOKENS,), 0, 1000)
    limits = 80 + 160 * jnp.arange(TOKENS, dtype=jnp.int32) // TOKENS
    return (rolls < limits).astype(jnp.int32)


def draw_width_params(key, part):
    key = jax.random.fold_in(key, 11)
    first_key, second_key = jax.random.split(key)
    biases = jnp.clip(jax.random.normal(first_key, (6, D), jnp.float32), -3.0, 3.0) * 0.3
    gains = 1.0 + 0.15 * jax.random.uniform(second_key, (6, D), jnp.float32, -1.0, 1.0)
    rows = jnp.arange(6, dtype=jnp.int32)[:, None]
    is_gain = (rows == 2) | (rows == 4)
    return jnp.where(is_gain, gains, biases).astype(jnp.float32)


def touch_ends(result, key, least, largest):
    longest = result.shape.index(max(result.shape))
    spots = []
    for shift in (0, 1):
        where = [jax.random.randint(jax.random.fold_in(key, axis), (), 0, length) for axis, length in enumerate(result.shape)]
        where[longest] = (where[longest] + shift) % result.shape[longest]
        spots.append(tuple(where))
    return result.at[spots[0]].set(least).at[spots[1]].set(largest)


def shard_levels(key, shape, cuts, smallest, high):
    def one(position, blocks):
        steps = jax.random.uniform(jax.random.fold_in(jax.random.fold_in(key, 6), position), (blocks,), jnp.float32, smallest / len(cuts), high / len(cuts))
        return jnp.repeat(jnp.exp(steps), shape[position] // blocks).reshape((-1,) + (1,) * (len(shape) - position - 1))

    level = one(*cuts[0])
    for cut in cuts[1:]:
        level = level * one(*cut)
    return level


def profile(amount, total, most, skew):
    weights = [(1 << 20) // math.isqrt(grade ** skew) + 1 for grade in range(2, amount + 1)]
    rest, given = total - most - (amount - 1), [1] * (amount - 1)
    while rest > 0:
        free = [i for i in range(amount - 1) if given[i] < most]
        pool, left = sum([weights[i] for i in free]), rest
        for i in free:
            addition = min(most - given[i], max(1, left * weights[i] // pool), rest)
            given[i] = given[i] + addition
            rest = rest - addition
    return np.array([most] + given)


def uneven(key, count, total, most, lean):
    if count == 2:
        one = jax.random.randint(key, (), max(1, total - most), min(most, total - 1) + 1)
        return jnp.stack([one, total - one])
    sizes = jnp.asarray(profile(count, total, most, lean), jnp.int32)
    twos = (count - 1) // 2
    giver, taker = sizes[1:1 + 2 * twos:2], sizes[2:2 + 2 * twos:2]
    slack = jnp.minimum(giver - 1, most - taker)
    passed = jax.random.randint(jax.random.fold_in(key, 1), (twos,), 0, 1 << 20) % (slack + 1)
    sizes = sizes.at[1:1 + 2 * twos:2].set(giver - passed).at[2:2 + 2 * twos:2].set(taker + passed)
    return sizes[jax.random.permutation(jax.random.fold_in(key, 2), count)]


def normal_values(own_key, shape, deviation, bound, cuts=(), kind=jnp.bfloat16):
    drawn = deviation * jax.random.normal(own_key, shape, jnp.float32)
    if cuts:
        drawn = drawn * shard_levels(own_key, shape, cuts, -0.22, 0.18)
    return jnp.clip(drawn, -bound, bound).astype(kind)


def setup_inputs(seed: int = 0) -> dict:
    key_list = jax.random.split(jax.random.key(seed), 25)
    inputs = normal_values(key_list[0], (TOKENS, D), 1.0, 6.0, ((0, 32),))
    cotangent = normal_values(key_list[1], (TOKENS, D), 1.0, 6.0, ((0, 32),))
    lengths = uneven(key_list[2], SEQS, TOKENS, LENGTH, 2).astype(jnp.int32)
    query_codes = touch_ends(jax.random.randint(key_list[3], (TOKENS, HASHES), 0, BUCKETS), jax.random.fold_in(key_list[3], 1), 0, BUCKETS - 1).astype(jnp.int32)
    key_codes = touch_ends(jax.random.randint(key_list[4], (TOKENS, HASHES), 0, BUCKETS), jax.random.fold_in(key_list[4], 1), 0, BUCKETS - 1).astype(jnp.int32)
    masked = draw_masked(jax.random.fold_in(key_list[24], 71), 0)
    entry_weight = normal_values(key_list[6], (D, 3, D), D ** -0.5, 0.21875, ((0, 32), (2, 4)), jnp.float32)
    entry_moment = normal_values(key_list[7], (D, 3, D), (0.5 * TOKENS ** 0.5), 448.0, ((0, 32), (2, 4)), jnp.float32)
    entry_square = jnp.clip(jnp.exp(math.log(24576.0) - 1.3862944 * jax.random.uniform(key_list[8], (D, 3, D), jnp.float32) ** shard_levels(key_list[8], (D, 3, D), ((0, 32), (2, 4)), -0.2, 0.2)), 6144.0, 24576.0)
    merge_weight = normal_values(key_list[9], (D, D), D ** -0.5, 0.21875, ((0, 4), (1, 32)), jnp.float32)
    merge_moment = normal_values(key_list[10], (D, D), (1.2 * TOKENS ** 0.5), 1024.0, ((0, 4), (1, 32)), jnp.float32)
    merge_square = jnp.clip(jnp.exp(math.log(147456.0) - 1.3862944 * jax.random.uniform(key_list[11], (D, D), jnp.float32) ** shard_levels(key_list[11], (D, D), ((0, 4), (1, 32)), -0.2, 0.2)), 36864.0, 147456.0)
    expand_weight = normal_values(key_list[12], (D, FF), D ** -0.5, 0.21875, ((0, 32), (1, 4)), jnp.float32)
    expand_moment = normal_values(key_list[13], (D, FF), (0.3 * TOKENS ** 0.5), 256.0, ((0, 32), (1, 4)), jnp.float32)
    expand_square = jnp.clip(jnp.exp(math.log(9830.4) - 1.3862944 * jax.random.uniform(key_list[14], (D, FF), jnp.float32) ** shard_levels(key_list[14], (D, FF), ((0, 32), (1, 4)), -0.2, 0.2)), 2457.6, 9830.4)
    reduce_weight = normal_values(key_list[15], (FF, D), FF ** -0.5, 0.109375, ((0, 4), (1, 32)), jnp.float32)
    reduce_moment = normal_values(key_list[16], (FF, D), (0.65 * TOKENS ** 0.5), 640.0, ((0, 4), (1, 32)), jnp.float32)
    reduce_square = jnp.clip(jnp.exp(math.log(39321.6) - 1.3862944 * jax.random.uniform(key_list[17], (FF, D), jnp.float32) ** shard_levels(key_list[17], (FF, D), ((0, 4), (1, 32)), -0.2, 0.2)), 9830.4, 39321.6)
    split_bias = normal_values(key_list[18], (H, 3 * DH + FF // H), 0.5, 3.0, ((0, 4), (1, 32)), jnp.float32)
    split_moment = normal_values(key_list[19], (H, 3 * DH + FF // H), (0.4 * TOKENS ** 0.5), 384.0, ((0, 4), (1, 32)), jnp.float32)
    split_square = jnp.clip(jnp.exp(math.log(9830.4) - 1.3862944 * jax.random.uniform(key_list[20], (H, 3 * DH + FF // H), jnp.float32) ** shard_levels(key_list[20], (H, 3 * DH + FF // H), ((0, 4), (1, 32)), -0.2, 0.2)), 2457.6, 9830.4)
    width_params = draw_width_params(jax.random.fold_in(key_list[24], 71), 0)
    width_moment = normal_values(key_list[22], (6, D), (1.0 * TOKENS ** 0.5), 896.0, ((1, 32),), jnp.float32)
    width_square = jnp.clip(jnp.exp(math.log(98304.0) - 1.3862944 * jax.random.uniform(key_list[23], (6, D), jnp.float32) ** shard_levels(key_list[23], (6, D), ((1, 32),), -0.2, 0.2)), 24576.0, 98304.0)
    return dict(inputs=inputs, cotangent=cotangent, lengths=lengths, query_codes=query_codes, key_codes=key_codes, masked=masked, entry_weight=entry_weight, entry_moment=entry_moment, entry_square=entry_square, merge_weight=merge_weight, merge_moment=merge_moment, merge_square=merge_square, expand_weight=expand_weight, expand_moment=expand_moment, expand_square=expand_square, reduce_weight=reduce_weight, reduce_moment=reduce_moment, reduce_square=reduce_square, split_bias=split_bias, split_moment=split_moment, split_square=split_square, width_params=width_params, width_moment=width_moment, width_square=width_square)


HIGHEST = lax.Precision.HIGHEST

@jax.custom_vjp
def low(v):
    return lax.optimization_barrier(v.astype(jnp.bfloat16)).astype(jnp.float32)

@jax.custom_vjp
def low_back(v):
    return v

def low_keep(v):
    return (low(v), None)

def low_pass(kept, grad):
    return (grad,)

def back_keep(v):
    return (v, None)

def back_low(kept, grad):
    return (low(grad),)
low.defvjp(low_keep, low_pass)
low_back.defvjp(back_keep, back_low)

def unit_rows(values):
    return values * lax.rsqrt(lax.optimization_barrier(jnp.sum(values * values, axis=-1, keepdims=True)) + 1e-06)

def norm_rows(rows, gain, shift):
    centre = rows - lax.optimization_barrier(jnp.mean(rows, axis=-1, keepdims=True))
    return centre * lax.rsqrt(lax.optimization_barrier(jnp.mean(centre * centre, axis=-1, keepdims=True)) + 1e-05) * gain + shift

def forward(inputs, entry, merging, expanding, reducing, split_bias, width_params, query_codes, key_codes, labels):
    total_tokens, width = inputs.shape
    heads = split_bias.shape[0]
    head_size = width // heads
    block_rows = total_tokens // N_SEQ
    window = block_rows + 2 * LENGTH
    entry_low = low(entry)
    merge_low = low(merging)
    expand_low = low(expanding)
    reduce_low = low(reducing)
    split_low = low(split_bias)
    width_low = low(width_params)
    entry_bias = split_low[:, :3 * head_size].reshape(heads, 3, head_size).transpose(1, 0, 2).reshape(3, width)
    expand_bias = split_low[:, 3 * head_size:].reshape(-1)
    projected = low_back(jnp.einsum('td,dce->tce', inputs, entry_low, precision=HIGHEST) + entry_bias)
    projected = projected.reshape(total_tokens, 3, heads, head_size)
    query = low(unit_rows(projected[:, 0]))
    key = low(unit_rows(projected[:, 1]))
    value = low(projected[:, 2])
    key_pad = jnp.pad(key, ((LENGTH, LENGTH), (0, 0), (0, 0)))
    value_pad = jnp.pad(value, ((LENGTH, LENGTH), (0, 0), (0, 0)))
    codes_pad = jnp.pad(key_codes, ((LENGTH, LENGTH), (0, 0)), constant_values=-1)
    labels_pad = jnp.pad(labels, (LENGTH, LENGTH), constant_values=-1)

    def block_fn(index):
        start = (index * block_rows).astype(jnp.int32)
        query_block = lax.dynamic_slice_in_dim(query, start, block_rows, 0)
        key_window = lax.dynamic_slice_in_dim(key_pad, start, window, 0)
        value_window = lax.dynamic_slice_in_dim(value_pad, start, window, 0)
        codes_query = lax.dynamic_slice_in_dim(query_codes, start, block_rows, 0)
        codes_window = lax.dynamic_slice_in_dim(codes_pad, start, window, 0)
        labels_query = lax.dynamic_slice_in_dim(labels, start, block_rows, 0)
        labels_window = lax.dynamic_slice_in_dim(labels_pad, start, window, 0)
        counts = jnp.zeros((block_rows, window), jnp.float32)
        for hash_index in range(HASHES):
            counts = counts + (codes_query[:, hash_index][:, None] == codes_window[:, hash_index][None, :]).astype(jnp.float32)
        counts = jnp.where(labels_query[:, None] == labels_window[None, :], counts, jnp.float32(0.0))

        def head_fn(parts):
            query_head, key_head, value_head = parts
            cosine = low_back(jnp.dot(query_head, key_head.T, precision=HIGHEST))
            kernel = low(counts / HASHES * ((1.0 + cosine) * 0.5) ** TAU)
            return jnp.dot(kernel, value_head, precision=HIGHEST)
        return lax.map(jax.checkpoint(head_fn), (query_block.transpose(1, 0, 2), key_window.transpose(1, 0, 2), value_window.transpose(1, 0, 2)))
    summed = lax.map(jax.checkpoint(block_fn), jnp.arange(N_SEQ, dtype=jnp.int32))
    summed = summed.transpose(0, 2, 1, 3).reshape(total_tokens, heads, head_size)
    summed = low_back(summed)
    mixed = low((summed * lax.rsqrt(lax.optimization_barrier(jnp.mean(summed * summed, axis=-1, keepdims=True)) + 1e-05)).reshape(total_tokens, width))
    attended = low_back(jnp.dot(mixed, merge_low, precision=HIGHEST) + width_low[0])
    hidden = norm_rows(inputs + attended, width_low[2], width_low[3])
    upper = low_back(jnp.dot(low(hidden), expand_low, precision=HIGHEST) + expand_bias)
    active = low(jax.nn.gelu(upper, approximate=False))
    fed = low_back(jnp.dot(active, reduce_low, precision=HIGHEST) + width_low[1])
    return norm_rows(hidden + fed, width_low[4], width_low[5])

def adamw(weight, moment, square, grad, rate):
    moment_new = 0.5 * moment + 0.5 * grad
    square_new = 0.5 * square + 0.5 * grad * grad
    fix = 1.0 - 0.5 ** STEP
    weight_new = weight - rate * (moment_new / fix / (jnp.sqrt(square_new / fix) + 1e-08) + 0.01 * weight)
    return (weight_new, moment_new, square_new)

def reference(inputs, cotangent, lengths, query_codes, key_codes, masked, entry_weight, entry_moment, entry_square, merge_weight, merge_moment, merge_square, expand_weight, expand_moment, expand_square, reduce_weight, reduce_moment, reduce_square, split_bias, split_moment, split_square, width_params, width_moment, width_square):
    endings = jnp.cumsum(lengths).astype(jnp.int32)
    positions = jnp.arange(TOKENS, dtype=jnp.int32)
    labels = lax.optimization_barrier(jnp.sum((positions[:, None] >= endings[None, :]).astype(jnp.int32), axis=1)).astype(jnp.int32)
    masked_float = masked.astype(jnp.float32)
    masked_total = jnp.sum(masked_float)
    grad_out = cotangent.astype(jnp.float32) * masked_float[:, None] * jnp.sqrt(TOKENS / (masked_total + 1.0))

    def layer_fn(inputs_float, entry, merging, expanding, reducing, splitting, widths):
        return forward(inputs_float, entry, merging, expanding, reducing, splitting, widths, query_codes, key_codes, labels)
    output, back = jax.vjp(layer_fn, inputs.astype(jnp.float32), entry_weight, merge_weight, expand_weight, reduce_weight, split_bias, width_params)
    grads = back(grad_out)
    entry_new = adamw(entry_weight, entry_moment, entry_square, grads[1], 0.02)
    merge_new = adamw(merge_weight, merge_moment, merge_square, grads[2], 0.02)
    expand_new = adamw(expand_weight, expand_moment, expand_square, grads[3], 0.02)
    reduce_new = adamw(reduce_weight, reduce_moment, reduce_square, grads[4], 0.02)
    split_new = adamw(split_bias, split_moment, split_square, grads[5], 0.5)
    width_new = adamw(width_params, width_moment, width_square, grads[6], 0.5)
    return (output.astype(jnp.bfloat16), grads[0], entry_new[0], entry_new[1], entry_new[2], merge_new[0], merge_new[1], merge_new[2], expand_new[0], expand_new[1], expand_new[2], reduce_new[0], reduce_new[1], reduce_new[2], split_new[0], split_new[1], split_new[2], width_new[0], width_new[1], width_new[2])
```

```python
import functools
import math

import jax
import jax.numpy as jnp
from jax import lax
from jax.experimental import pallas as pl
from jax.experimental.pallas import tpu as pltpu
from jax.sharding import PartitionSpec as P

DH = 64
HASHES = 32
STEP = 10
LENGTH = 4096
QUERY_TILE = 384
KEY_TILE = 256
ROW_TILE = 256
WIDTH_LANE = 48
SECOND_AFTER = 2
PLANES = 8

UNIT_EPS = 1e-06
NORM_EPS = 1e-05
BETA = 0.5
MATRIX_RATE = 0.02
VECTOR_RATE = 0.5
DECAY = 0.01
ADAM_EPS = 1e-08

f32 = jnp.float32
bf16 = jnp.bfloat16
i32 = jnp.int32


def dot_nt(a, b):
    return lax.dot_general(a, b, (((1,), (1,)), ((), ())), preferred_element_type=f32)


def dot_nn(a, b):
    return lax.dot_general(a, b, (((1,), (0,)), ((), ())), preferred_element_type=f32)


def dot_tn(a, b):
    return lax.dot_general(a, b, (((0,), (0,)), ((), ())), preferred_element_type=f32)


def kernel_call(kernel, outs, operands, scratch=(), smem=0, flops=10**9, name=None):
    spaces = [pltpu.SMEM] * smem + [pltpu.VMEM] * (len(operands) - smem)
    return pl.pallas_call(
        kernel,
        out_shape=[jax.ShapeDtypeStruct(shape, kind) for shape, kind in outs],
        in_specs=[pl.BlockSpec(memory_space=space) for space in spaces],
        out_specs=[pl.BlockSpec(memory_space=pltpu.VMEM)] * len(outs),
        scratch_shapes=list(scratch),
        compiler_params=pltpu.CompilerParams(vmem_limit_bytes=44 * 2**20),
        cost_estimate=pl.CostEstimate(
            flops=flops,
            bytes_accessed=sum(o.size * o.dtype.itemsize for o in operands),
            transcendentals=0,
        ),
        name=name,
    )(*operands)


def row_tiles(total):
    return [slice(r, r + ROW_TILE) for r in range(0, total, ROW_TILE)]


def left_half(rows):
    return lax.broadcasted_iota(i32, (rows, 2 * DH), 1) < DH


def half_sum(values, mask):
    return jnp.sum(jnp.where(mask, values, 0.0), axis=-1, keepdims=True)


def endings_of(len_ref):
    out = []
    total = jnp.int32(0)
    for s in range(len_ref.shape[0]):
        total = total + len_ref[s]
        out.append(total)
    return out


def labels_of(positions, ends):
    total = jnp.zeros(positions.shape, i32)
    for end in ends:
        total = total + (positions >= end).astype(i32)
    return total


def reach_of(first, last, ends):
    begin = jnp.int32(0)
    finish = jnp.int32(0)
    previous = jnp.int32(0)
    for end in ends:
        begin = jnp.where((first >= previous) & (first < end), previous, begin)
        finish = jnp.where((last >= previous) & (last < end), end, finish)
        previous = end
    return begin, finish


def pair_matches(wide, lane_planes, row_labels, lane_labels):
    parts = []
    for part in range(lane_planes.shape[1] // 128):
        lanes = slice(part * 128, part * 128 + 128)
        same = wide[0] ^ lane_planes[0:1, lanes]
        for b in range(1, PLANES):
            same = same & (wide[b] ^ lane_planes[b : b + 1, lanes])
        parts.append(same)
    matches = lax.population_count(jnp.concatenate(parts, axis=1))
    return jnp.where(row_labels == lane_labels, matches, 0).astype(f32)


def planes_of(codes):
    place = lax.broadcasted_iota(i32, codes.shape, 0)
    rows = []
    for b in range(PLANES):
        bits = ((codes >> b) & 1) << place
        part = bits[0:8] | bits[8:16] | bits[16:24] | bits[24:32]
        part = part | pltpu.roll(part, 4, 0)
        part = part | pltpu.roll(part, 2, 0)
        part = part | pltpu.roll(part, 1, 0)
        rows.append(part[0:1])
    return jnp.concatenate(rows, axis=0)


def block_planes(payload, rows, planes):
    width = payload.shape[1]
    for first in range(0, rows, width):
        place = rows + first // width * HASHES
        codes = payload[place : place + HASHES, :].astype(f32).astype(i32)
        size = min(width, rows - first)
        planes[:, first : first + size] = ~planes_of(codes[:, :size])


def attend_kernel(slots, len_ref, here_ref, query, own_planes, *refs):
    count = len(slots)
    payloads, refs = refs[:count], refs[count:]
    before = None
    if len(refs) == 4 + count:
        before, refs = refs[0], refs[1:]
    out, wide, total, planes = refs[0], refs[1], refs[2], refs[3:]
    block_rows, width = query.shape
    heads = width // 128
    ends = endings_of(len_ref)
    here = here_ref[0] * block_rows
    for (_, _, sent), payload, plane in zip(slots, payloads, planes):
        block_planes(payload, sent, plane)

    def own_tile(own, carry):
        rows = pl.ds(pl.multiple_of(own * QUERY_TILE, QUERY_TILE), QUERY_TILE)
        for b in range(PLANES):
            wide[b] = jnp.broadcast_to(own_planes[rows, b : b + 1], (QUERY_TILE, 128))
        total[...] = jnp.zeros_like(total)
        first = here + own * QUERY_TILE
        begin, finish = reach_of(first, first + (QUERY_TILE - 1), ends)
        row_labels = labels_of(first + lax.broadcasted_iota(i32, (QUERY_TILE, 1), 0), ends)
        for (offset, skipped, sent), keyval, plane in zip(slots, payloads, planes):
            start = here + offset * block_rows + skipped
            tiles = sent // KEY_TILE
            low = jnp.clip((begin - start) // KEY_TILE, 0, tiles)
            high = jnp.clip((finish - start + (KEY_TILE - 1)) // KEY_TILE, 0, tiles)

            def add_tile(tile, carry, start=start, keyval=keyval, plane=plane):
                place = pl.ds(pl.multiple_of(tile * KEY_TILE, KEY_TILE), KEY_TILE)
                lane_labels = labels_of(
                    start + tile * KEY_TILE + lax.broadcasted_iota(i32, (1, KEY_TILE), 1), ends
                )
                matches = pair_matches(wide, plane[:, place], row_labels, lane_labels)
                for h in range(heads):
                    lanes = slice(h * 128, h * 128 + 128)
                    pairs = keyval[place, lanes]
                    base = dot_nt(query[rows, lanes], pairs) + 1.0
                    base = base * base
                    base = base * base
                    total[:, lanes] += dot_nn((matches * (base * base)).astype(bf16), pairs)
                return carry

            lax.fori_loop(low, high, add_tile, 0)
        result = total[...] * (1.0 / (HASHES * 256.0))
        out[rows, :] = result if before is None else before[rows, :] + result
        return carry

    lax.fori_loop(0, block_rows // QUERY_TILE, own_tile, 0)


def back_kernel(slots, len_ref, here_ref, query, upstream, own_planes, *refs):
    count = len(slots)
    payloads, refs = refs[:count], refs[count:]
    before = None
    if len(refs) == 3 + 2 * count + 1:
        before, refs = refs[0], refs[1:]
    outs, query_out, wide, total = refs[:count], refs[count], refs[count + 1], refs[count + 2]
    planes = refs[count + 3 :]
    block_rows, width = query.shape
    heads = width // 128
    ends = endings_of(len_ref)
    here = here_ref[0] * block_rows
    tiles = block_rows // QUERY_TILE
    query_out[...] = jnp.zeros_like(query_out) if before is None else before[...]
    for (_, _, sent), payload, plane in zip(slots, payloads, planes):
        block_planes(payload, sent, plane)
    for (offset, skipped, sent), keyval, plane, out in zip(slots, payloads, planes, outs):

        def key_tile(part, carry, offset=offset, skipped=skipped, keyval=keyval, plane=plane, out=out):
            rows = pl.ds(pl.multiple_of(part * KEY_TILE, KEY_TILE), KEY_TILE)
            start = here + offset * block_rows + skipped + part * KEY_TILE
            begin, finish = reach_of(start, start + (KEY_TILE - 1), ends)
            low = jnp.clip((begin - here) // QUERY_TILE, 0, tiles)
            high = jnp.clip((finish - here + (QUERY_TILE - 1)) // QUERY_TILE, 0, tiles)
            total[...] = jnp.zeros_like(total)

            @pl.when(low < high)
            def _():
                columns = jnp.transpose(plane[:, rows])
                for b in range(PLANES):
                    wide[b] = jnp.broadcast_to(columns[:, b : b + 1], (KEY_TILE, 128))
                row_labels = labels_of(start + lax.broadcasted_iota(i32, (KEY_TILE, 1), 0), ends)

                def add_tile(tile, carry):
                    place = pl.ds(pl.multiple_of(tile * QUERY_TILE, QUERY_TILE), QUERY_TILE)
                    lane_labels = labels_of(
                        here + tile * QUERY_TILE + lax.broadcasted_iota(i32, (1, QUERY_TILE), 1), ends
                    )
                    matches = pair_matches(wide, own_planes[:, place], row_labels, lane_labels)
                    for h in range(heads):
                        lanes = slice(h * 128, h * 128 + 128)
                        pairs = keyval[rows, lanes]
                        asking = query[place, lanes]
                        arriving = upstream[place, lanes]
                        base = dot_nt(pairs, asking) + 1.0
                        grad = dot_nt(pairs, arriving)
                        square = base * base
                        power = matches * ((square * square) * (square * base))
                        grad_low = (grad * power).astype(bf16)
                        total[0, :, lanes] += dot_nn(grad_low, asking)
                        total[1, :, lanes] += dot_nn((power * base).astype(bf16), arriving)
                        query_out[place, lanes] += dot_tn(grad_low, pairs) * (4.0 / (HASHES * 128.0))
                    return carry

                lax.fori_loop(low, high, add_tile, 0)

            out[rows, :] = (
                total[0] * (4.0 / (HASHES * 128.0)) + total[1] * (1.0 / (HASHES * 256.0))
            ).astype(out.dtype)
            return carry

        lax.fori_loop(0, sent // KEY_TILE, key_tile, 0)


def attend(slots, lengths, here, query, own_planes, payloads, before):
    block_rows, width = query.shape
    operands = [lengths, here, query, own_planes, *payloads]
    if before is not None:
        operands.append(before)
    return kernel_call(
        functools.partial(attend_kernel, slots),
        [((block_rows, width), f32)],
        operands,
        scratch=[pltpu.VMEM((PLANES, QUERY_TILE, 128), i32), pltpu.VMEM((QUERY_TILE, width), f32)]
        + [pltpu.VMEM((PLANES, sent), i32) for _, _, sent in slots],
        smem=2,
        flops=sum(sent for _, _, sent in slots) * block_rows * 100,
        name="attend",
    )[0]


def attend_back(slots, lengths, here, query, upstream, own_planes, payloads, before):
    block_rows, width = query.shape
    operands = [lengths, here, query, upstream, own_planes, *payloads]
    if before is not None:
        operands.append(before)
    *parts, total = kernel_call(
        functools.partial(back_kernel, slots),
        [((sent, width), bf16) for _, _, sent in slots] + [((block_rows, width), f32)],
        operands,
        scratch=[pltpu.VMEM((PLANES, KEY_TILE, 128), i32), pltpu.VMEM((2, KEY_TILE, width), f32)]
        + [pltpu.VMEM((PLANES, sent), i32) for _, _, sent in slots],
        smem=2,
        flops=sum(sent for _, _, sent in slots) * block_rows * 200,
        name="attend_back",
    )
    return parts, total


def project_kernel(inputs, weights, bias, query_codes, key_codes, raw, query, payload, head, tail, lanes, columns):
    block_rows = inputs.shape[0]
    width = query.shape[1]
    heads = width // 128
    edge = head.shape[0] - HASHES
    left = left_half(ROW_TILE)
    for rows in row_tiles(block_rows):
        values = dot_nn(inputs[rows, :], weights[:, : 2 * width]) + bias[...]
        raw[rows, :] = values
        for h in range(heads):
            pair = values[:, h * 128 : h * 128 + 128]
            inverse = lax.rsqrt(half_sum(pair * pair, left) + UNIT_EPS)
            payload[rows, h * 128 : h * 128 + 128] = jnp.where(left, pair * inverse, pair).astype(bf16)
            asking = values[:, width + h * 128 : width + h * 128 + 128]
            inverse = lax.rsqrt(half_sum(asking * asking, left) + UNIT_EPS)
            query[rows, h * 128 : h * 128 + 128] = jnp.where(left, asking * inverse, 0.0).astype(bf16)
    codes = key_codes[...].astype(f32).astype(bf16)
    for first in range(0, block_rows, width):
        place = block_rows + first // width * HASHES
        payload[place : place + HASHES, :] = codes[:, first : first + width]
    head[0:edge, :] = payload[0:edge, :]
    tail[0:edge, :] = payload[block_rows - edge : block_rows, :]
    rest = jnp.zeros((HASHES, width - edge), bf16)
    head[edge:, :] = jnp.concatenate([codes[:, :edge], rest], axis=1)
    tail[edge:, :] = jnp.concatenate([codes[:, block_rows - edge :], rest], axis=1)
    planes = planes_of(query_codes[...])
    lanes[...] = planes
    for rows in row_tiles(block_rows):
        columns[rows, :] = jnp.transpose(planes[:, rows])


def mix_kernel(summed, weights, mixed, part):
    width = summed.shape[1]
    right = ~left_half(ROW_TILE)
    for rows in row_tiles(summed.shape[0]):
        for h in range(width // 128):
            lanes = slice(h * 128, h * 128 + 128)
            values = summed[rows, lanes]
            inverse = lax.rsqrt(half_sum(values * values, right) * (1.0 / DH) + NORM_EPS)
            mixed[rows, lanes] = jnp.where(right, values * inverse, 0.0).astype(bf16)
        part[rows, :] = dot_nt(mixed[rows, :], weights[:, width : 2 * width])


def row_mean(values):
    return jnp.sum(values, axis=-1, keepdims=True) * (1.0 / values.shape[-1])


def feed_kernel(inputs, attended, vectors, weights, bias, hidden, normed, inverse, active, slope, part):
    units = bias.shape[1]
    for rows in row_tiles(inputs.shape[0]):
        values = inputs[rows, :].astype(f32) + (attended[rows, :].astype(f32) + vectors[0:1, :])
        centre = values - row_mean(values)
        scale = lax.rsqrt(row_mean(centre * centre) + NORM_EPS)
        unit = centre * scale
        result = unit * vectors[2:3, :] + vectors[3:4, :]
        normed[rows, :] = unit
        inverse[rows, :] = scale
        hidden[rows, :] = result
        upper = dot_nn(result.astype(bf16), weights[:, :units]) + bias[...]
        curve = 0.5 * (1.0 + lax.erf(upper * math.sqrt(0.5)))
        active[rows, :] = (upper * curve).astype(bf16)
        slope[rows, :] = curve + upper * (jnp.exp(-0.5 * upper * upper) * (1.0 / math.sqrt(2.0 * math.pi)))
        part[rows, :] = dot_nt(active[rows, :], weights[:, units:])


def feed_back_kernel(hidden, fed, cotangent, scale, vectors, weights, active, slope, out, second, part, grads, width_sums, unit_sums, total):
    units = active.shape[1]
    total[...] = jnp.zeros_like(total)
    sums = [0.0, 0.0, 0.0]
    unit_sum = 0.0
    for rows in row_tiles(hidden.shape[0]):
        low = hidden[rows, :]
        values = low + (fed[rows, :].astype(f32) + vectors[1:2, :])
        centre = values - row_mean(values)
        inverse = lax.rsqrt(row_mean(centre * centre) + NORM_EPS)
        normed = centre * inverse
        out[rows, :] = (normed * vectors[4:5, :] + vectors[5:6, :]).astype(bf16)
        upstream = cotangent[rows, :].astype(f32) * scale[rows, :]
        sums[1] += jnp.sum(upstream * normed, axis=0, keepdims=True)
        sums[2] += jnp.sum(upstream, axis=0, keepdims=True)
        scaled = upstream * vectors[4:5, :]
        grad = inverse * (scaled - row_mean(scaled) - normed * row_mean(scaled * normed))
        second[rows, :] = grad
        grad_low = grad.astype(bf16)
        sums[0] += jnp.sum(grad_low.astype(f32), axis=0, keepdims=True)
        upper = (dot_nn(grad_low, weights[:, units:]) * slope[rows, :]).astype(bf16)
        unit_sum += jnp.sum(upper.astype(f32), axis=0, keepdims=True)
        part[rows, :] = dot_nt(upper, weights[:, :units])
        total[:, :units] += dot_tn(low.astype(bf16), upper)
        total[:, units:] += dot_tn(grad_low, active[rows, :])
    grads[...] = total[...].astype(bf16)
    width_sums[...] = jnp.concatenate(sums, axis=0)
    unit_sums[...] = unit_sum


def mix_back_kernel(second, came, normed, inverse, vectors, weights, mixed, summed, first, upstream, grads, width_sums, total):
    width = summed.shape[1]
    right = ~left_half(ROW_TILE)
    total[...] = jnp.zeros_like(total)
    sums = [0.0, 0.0, 0.0]
    for rows in row_tiles(second.shape[0]):
        hidden = second[rows, :] + came[rows, :].astype(f32)
        unit = normed[rows, :]
        sums[1] += jnp.sum(hidden * unit, axis=0, keepdims=True)
        sums[2] += jnp.sum(hidden, axis=0, keepdims=True)
        scaled = hidden * vectors[2:3, :]
        grad = inverse[rows, :] * (scaled - row_mean(scaled) - unit * row_mean(scaled * unit))
        first[rows, :] = grad
        grad_low = grad.astype(bf16)
        sums[0] += jnp.sum(grad_low.astype(f32), axis=0, keepdims=True)
        total[...] += dot_tn(grad_low, mixed[rows, :])
        arriving = dot_nn(grad_low, weights[:, width : 2 * width])
        for h in range(width // 128):
            lanes = slice(h * 128, h * 128 + 128)
            values = summed[rows, lanes]
            scale = lax.rsqrt(half_sum(values * values, right) * (1.0 / DH) + NORM_EPS)
            unit = values * scale
            piece = arriving[:, lanes]
            mean = half_sum(piece * unit, right) * (1.0 / DH)
            upstream[rows, lanes] = jnp.where(right, scale * (piece - unit * mean), 0.0).astype(bf16)
    grads[...] = total[...].astype(bf16)
    width_sums[...] = jnp.concatenate(sums, axis=0)


def project_back_kernel(count, ranks, inputs, weights, raw, query_grad, merge_grads, unit_sums, width_sums, *refs):
    parts, (part, grads, total) = refs[:count], refs[count:]
    block_rows, width = query_grad.shape
    left = left_half(ROW_TILE)
    total[...] = jnp.zeros_like(total)
    column_sum = 0.0
    for rows in row_tiles(block_rows):
        pieces = []
        for h in range(width // 128):
            lanes = slice(h * 128, h * 128 + 128)
            came = 0.0
            for ref in parts:
                sent = ref.shape[0] if ref.shape[0] == block_rows else None
                if sent is not None:
                    came = came + ref[rows, lanes].astype(f32)
            if rows.start == 0:
                came = came + parts[count - 2][:, lanes].astype(f32)
            if rows.stop == block_rows:
                came = came + parts[count - 1][:, lanes].astype(f32)
            values = raw[rows, lanes]
            scale = lax.rsqrt(half_sum(values * values, left) + UNIT_EPS)
            unit = values * scale
            along = half_sum(came * unit, left)
            pieces.append(jnp.where(left, scale * (came - unit * along), came).astype(bf16))
        for h in range(width // 128):
            lanes = slice(h * 128, h * 128 + 128)
            values = raw[rows, width + h * 128 : width + h * 128 + 128]
            scale = lax.rsqrt(half_sum(values * values, left) + UNIT_EPS)
            unit = values * scale
            came = query_grad[rows, lanes]
            along = half_sum(came * unit, left)
            pieces.append(jnp.where(left, scale * (came - unit * along), 0.0).astype(bf16))
        projected = jnp.concatenate(pieces, axis=1)
        column_sum += jnp.sum(projected.astype(f32), axis=0, keepdims=True)
        part[rows, :] = dot_nt(projected, weights[:, : 2 * width])
        total[...] += dot_tn(inputs[rows, :], projected)
    grads[:, :width] = total[:, :width].astype(bf16)
    grads[:, width : 2 * width] = (total[:, width:] + merge_grads[...].astype(f32)).astype(bf16)
    model_width = grads.shape[0]
    heads = width // (2 * DH)
    units = unit_sums.shape[1] // heads
    share = (3 * DH + units) // ranks
    spread = 0.0
    sources = [(column_sum, width + 2 * DH * h, 0, h, DH) for h in range(heads)]
    sources += [(column_sum, 2 * DH * h, DH, h, 2 * DH) for h in range(heads)]
    sources += [(unit_sums[...], units * h, 3 * DH, h, units) for h in range(heads)]
    for values, first, place, h, size in sources:
        size = size if size > DH else 2 * DH
        row = values[:, first : first + size]
        at = place + lax.broadcasted_iota(i32, (1, size), 1)
        if place == 0:
            row = jnp.where(at < DH, row, 0.0)
        owner = lax.broadcasted_iota(i32, (ranks, size), 0)
        picked = jnp.where((at >= owner * share) & (at < owner * share + share), row, 0.0)
        lane = lax.broadcasted_iota(i32, (size, 128), 1)
        source = place + lax.broadcasted_iota(i32, (size, 128), 0)
        moved = (lane - h * share == source % share) & (lane >= h * share) & (lane < h * share + share)
        spread = spread + dot_nn(picked.astype(bf16), moved.astype(f32).astype(bf16))
    rank_row = lax.broadcasted_iota(i32, (model_width, ranks), 0)
    rank = lax.broadcasted_iota(i32, (model_width, ranks), 1)
    where_to = (rank_row == rank * (model_width // ranks)).astype(f32).astype(bf16)
    lane = lax.broadcasted_iota(i32, (8, 128), 1)
    vector = lax.broadcasted_iota(i32, (8, 128), 0)
    vector_lane = ((lane == vector + WIDTH_LANE) & (vector < 6)).astype(f32).astype(bf16)
    grads[:, 2 * width :] = (
        dot_nn(where_to, spread.astype(bf16)) + dot_tn(width_sums[...].astype(bf16), vector_lane)
    ).astype(bf16)


def unpair(both):
    width = both.shape[1]
    first = [both[:, w : w + DH] for w in range(0, width, 2 * DH)]
    second = [both[:, w + DH : w + 2 * DH] for w in range(0, width, 2 * DH)]
    return jnp.concatenate(first, axis=1), jnp.concatenate(second, axis=1)


def update(grad, state, outs, rate, place=Ellipsis):
    weight, moment, square = (ref[place] for ref in state)
    moment_new = BETA * moment + (1.0 - BETA) * grad
    square_new = BETA * square + (1.0 - BETA) * grad * grad
    fix = 1.0 - BETA**STEP
    outs[0][place] = weight - rate * (
        moment_new * (1.0 / fix) / (jnp.sqrt(square_new * (1.0 / fix)) + ADAM_EPS) + DECAY * weight
    )
    outs[1][place] = moment_new
    outs[2][place] = square_new


def sum_of(parts):
    total = parts[0].astype(f32)
    for index in range(1, parts.shape[0]):
        total = total + parts[index].astype(f32)
    return total


def finish_first_kernel(parts, *refs):
    state, outs = refs[:12], refs[12:]
    total = sum_of(parts)
    width = state[3].shape[0]
    key, value = unpair(total[:, : 2 * width])
    query, merge = unpair(total[:, 2 * width : 4 * width])
    for which, grad in enumerate((query, key, value)):
        update(grad, state[0:3], outs[0:3], MATRIX_RATE, (slice(None), which))
    update(jnp.transpose(merge), state[3:6], outs[3:6], MATRIX_RATE)
    rest = total[:, 4 * width :]
    size = state[6].shape[1]
    for row in range(state[6].shape[0]):
        update(rest[0:1, row * size : row * size + size], state[6:9], outs[6:9], VECTOR_RATE, (slice(row, row + 1), slice(None)))
    update(jnp.transpose(rest)[WIDTH_LANE : WIDTH_LANE + 6, :], state[9:12], outs[9:12], VECTOR_RATE)


def finish_second_kernel(parts, *refs):
    state, outs = refs[:6], refs[6:]
    total = sum_of(parts)
    units = state[0].shape[1]
    update(total[:, :units], state[0:3], outs[0:3], MATRIX_RATE)
    update(jnp.transpose(total[:, units:]), state[3:6], outs[3:6], MATRIX_RATE)


def shifted(value, steps):
    count = lax.axis_size("seq")
    return lax.ppermute(
        value, "seq", [(i, i + steps) for i in range(count) if 0 <= i + steps < count]
    )


def gather_rows(shard):
    count = lax.axis_size("seq")
    sent = jnp.broadcast_to(shard[None], (count,) + shard.shape)
    return lax.all_to_all(sent, "seq", 0, 0, tiled=True)


def scatter_rows(grads):
    count = lax.axis_size("seq")
    sent = grads.astype(bf16).reshape((count, grads.shape[0] // count) + grads.shape[1:])
    return lax.all_to_all(sent, "seq", 0, 0, tiled=True)


def swapped(value, mask):
    return lax.ppermute(value, "tp", [(i, i ^ mask) for i in range(lax.axis_size("tp"))])


def sum_over_tp(part):
    half = part.shape[0] // 2
    core = lax.axis_index("tp") % 2
    mine = lax.dynamic_slice_in_dim(part, core * half, half, 0)
    theirs = lax.dynamic_slice_in_dim(part, (1 - core) * half, half, 0).astype(bf16)
    here = (mine + swapped(theirs, 1).astype(f32)).astype(bf16)
    there = swapped(here, 2)
    total = (here.astype(f32) + there.astype(f32)).astype(bf16)
    other = swapped(total, 1)
    first = jnp.where(core == 0, total, other)
    second = jnp.where(core == 0, other, total)
    return jnp.concatenate([first, second], axis=0)


def paired(first, second):
    rows = first.shape[0]
    both = jnp.stack([first.reshape(rows, -1, DH), second.reshape(rows, -1, DH)], axis=2)
    return both.reshape(rows, -1)


def unpaired(both):
    rows = both.shape[0]
    split = both.reshape(rows, -1, 2, DH)
    return split[:, :, 0].reshape(rows, -1), split[:, :, 1].reshape(rows, -1)


def per_device(
    inputs,
    cotangent,
    lengths,
    query_codes,
    key_codes,
    masked,
    entry_weight,
    entry_moment,
    entry_square,
    merge_weight,
    merge_moment,
    merge_square,
    expand_weight,
    expand_moment,
    expand_square,
    reduce_weight,
    reduce_moment,
    reduce_square,
    split_bias,
    split_moment,
    split_square,
    width_params,
    width_moment,
    width_square,
):
    block_rows, model_width = inputs.shape
    count = lax.axis_size("seq")
    total_tokens = block_rows * count
    reach = (LENGTH - 2) // block_rows + 1
    heads = split_bias.shape[0]
    local = heads * DH
    shard_rows = model_width // count
    hidden_units = expand_weight.shape[1]
    split_columns = split_bias.shape[1]
    here_index = lax.axis_index("seq")
    here = here_index.astype(i32).reshape(1)

    masked_float = masked.astype(f32)
    masked_here = jnp.sum(masked)
    entry_shard = entry_weight.astype(bf16)
    split_flat = split_bias.astype(bf16).reshape(-1)
    split_pairs = jnp.pad(split_flat, (0, 2 * shard_rows - split_flat.shape[0]))
    counted = jnp.stack([masked_here // 256, masked_here % 256]).astype(bf16)
    extra = 4 * local
    first_shard = jnp.concatenate(
        [
            paired(entry_shard[:, 1], entry_shard[:, 2]),
            paired(entry_shard[:, 0], merge_weight.astype(bf16).T),
            width_params.astype(bf16).T,
            split_pairs.reshape(shard_rows, 2),
            jnp.pad(counted, (0, shard_rows - 2))[:, None],
            jnp.zeros((shard_rows, 119), bf16),
        ],
        axis=1,
    )
    first_full = gather_rows(first_shard)
    second_shard = jnp.concatenate(
        [expand_weight.astype(bf16), reduce_weight.astype(bf16).T], axis=1
    )
    weights = first_full.reshape(model_width, -1)
    vectors = first_full[:, :, extra : extra + 6].reshape(model_width, 6).T.astype(f32)
    split_float = (
        first_full[:, :, extra + 6 : extra + 8]
        .reshape(count, 2 * shard_rows)[:, : heads * split_columns]
        .reshape(count, heads, split_columns)
        .transpose(1, 0, 2)
        .reshape(heads, -1)
        .astype(f32)
    )
    masked_parts = first_full[:, :2, extra + 8].astype(f32)
    masked_total = jnp.sum(masked_parts[:, 0] * 256.0 + masked_parts[:, 1])
    scale = masked_float[:, None] * jnp.sqrt(total_tokens / (masked_total + 1.0))
    entry_bias = split_float[:, : 3 * DH].reshape(heads, 3, DH)
    entry_bias = jnp.concatenate(
        [
            paired(entry_bias[:, 1].reshape(1, -1), entry_bias[:, 2].reshape(1, -1)),
            paired(entry_bias[:, 0].reshape(1, -1), jnp.zeros((1, local), f32)),
        ],
        axis=1,
    )
    expand_bias = split_float[:, 3 * DH :].reshape(1, -1)

    far = KEY_TILE * -(-(LENGTH - 1 - (reach - 1) * block_rows) // KEY_TILE)
    slots = {0: (0, 0, block_rows)}
    for distance in range(1, reach):
        slots[distance] = (distance, 0, block_rows)
        slots[-distance] = (-distance, 0, block_rows)
    slots[reach] = (reach, 0, far)
    slots[-reach] = (-reach, block_rows - far, far)
    groups = [(0,), (-1, 1, -2, 2), (-3, 3, -4, 4), (-5, 5, -reach, reach)]

    pair_width = 2 * local
    code_rows = HASHES * -(-block_rows // pair_width)
    raw, query, whole, head, tail, query_lanes, query_columns = kernel_call(
        project_kernel,
        [
            ((block_rows, 2 * pair_width), f32),
            ((block_rows, pair_width), bf16),
            ((block_rows + code_rows, pair_width), bf16),
            ((far + HASHES, pair_width), bf16),
            ((far + HASHES, pair_width), bf16),
            ((PLANES, block_rows), i32),
            ((block_rows, PLANES), i32),
        ],
        [inputs, weights, entry_bias, query_codes.T, key_codes.T],
        flops=6 * 10**9,
        name="project",
    )
    near = {0: whole}
    summed = None
    second_full = None
    sources = (whole, head, tail)
    for number, offsets in enumerate(groups):
        if number + 1 < len(groups):
            for o in groups[number + 1]:
                near[o] = shifted({reach: sources[1], -reach: sources[2]}.get(o, sources[0]), -o)
        if number == SECOND_AFTER:
            second_shard, near[offsets[0]] = lax.optimization_barrier((second_shard, near[offsets[0]]))
            second_full = gather_rows(second_shard).reshape(model_width, -1)
        chosen = tuple(slots[o] for o in offsets)
        summed = attend(
            chosen, lengths, here, query, query_columns, [near[o] for o in offsets], summed
        )
        if number == 0:
            *sources, summed = lax.optimization_barrier((*sources, summed))
        elif number + 2 < len(groups):
            *sources, near[offsets[0]] = lax.optimization_barrier((*sources, near[offsets[0]]))

    square = (block_rows, model_width)
    mixed, part = kernel_call(
        mix_kernel,
        [((block_rows, pair_width), bf16), (square, f32)],
        [summed, weights],
        flops=3 * 10**9,
        name="mix",
    )
    attended = sum_over_tp(part)
    hidden, normed, inverse, active, slope, part = kernel_call(
        feed_kernel,
        [
            (square, f32),
            (square, f32),
            ((block_rows, 1), f32),
            ((block_rows, hidden_units), bf16),
            ((block_rows, hidden_units), f32),
            (square, f32),
        ],
        [inputs, attended, vectors, second_full, expand_bias],
        flops=8 * 10**9,
        name="feed",
    )
    fed = sum_over_tp(part)

    layer_out, grad_second, part, second_grads, second_sums, unit_sums = kernel_call(
        feed_back_kernel,
        [
            (square, bf16),
            (square, f32),
            (square, f32),
            ((model_width, 2 * hidden_units), bf16),
            ((3, model_width), f32),
            ((1, hidden_units), f32),
        ],
        [hidden, fed, cotangent, scale, vectors, second_full, active, slope],
        scratch=[pltpu.VMEM((model_width, 2 * hidden_units), f32)],
        flops=10 * 10**9,
        name="feed_back",
    )
    came = sum_over_tp(part)
    second_parts = scatter_rows(second_grads)
    second_states = [
        expand_weight, expand_moment, expand_square, reduce_weight, reduce_moment, reduce_square,
    ]
    second_finished = kernel_call(
        finish_second_kernel,
        [(state.shape, f32) for state in second_states],
        [second_parts] + second_states,
        flops=10**8,
        name="finish_second",
    )
    grad_first, upstream, merge_grads, first_sums = kernel_call(
        mix_back_kernel,
        [
            (square, f32),
            ((block_rows, pair_width), bf16),
            ((model_width, pair_width), bf16),
            ((3, model_width), f32),
        ],
        [grad_second, came, normed, inverse, vectors, weights, mixed, summed],
        scratch=[pltpu.VMEM((model_width, pair_width), f32)],
        flops=6 * 10**9,
        name="mix_back",
    )
    grad_query = None
    returned = {}
    waiting = []
    for offsets in reversed(groups):
        chosen = tuple(slots[o] for o in offsets)
        parts, grad_query = attend_back(
            chosen, lengths, here, query, upstream, query_lanes, [near[o] for o in offsets], grad_query
        )
        for o, piece in zip(offsets, parts):
            returned[o] = piece if o == 0 else shifted(piece, o)
        if waiting and 0 not in offsets:
            *arrived, grad_query = lax.optimization_barrier((*[returned[o] for o in waiting], grad_query))
            returned.update(zip(waiting, arrived))
        waiting = offsets
    *second_finished, grad_query = lax.optimization_barrier((*second_finished, grad_query))
    order = sorted(set(returned) - {reach, -reach}, key=abs) + [reach, -reach]
    width_sums = jnp.concatenate(
        [first_sums[:1], second_sums[:1], first_sums[1:], second_sums[1:], jnp.zeros((2, model_width), f32)]
    )
    part, first_grads = kernel_call(
        functools.partial(project_back_kernel, len(order), count),
        [(square, f32), ((model_width, 2 * pair_width + 128), bf16)],
        [inputs, weights, raw, grad_query, merge_grads, unit_sums, width_sums]
        + [returned[o] for o in order],
        scratch=[pltpu.VMEM((model_width, 2 * pair_width), f32)],
        flops=8 * 10**9,
        name="project_back",
    )
    input_sum = sum_over_tp(part)
    first_parts = scatter_rows(first_grads)
    input_grad = grad_first + input_sum.astype(f32)
    states = [
        entry_weight, entry_moment, entry_square, merge_weight, merge_moment, merge_square,
        split_bias, split_moment, split_square, width_params, width_moment, width_square,
    ]
    finished = kernel_call(
        finish_first_kernel,
        [(state.shape, f32) for state in states],
        [first_parts] + states,
        flops=10**8,
        name="finish_first",
    )
    return (layer_out, input_grad, *finished[:6], *second_finished, *finished[6:])


def solution(mesh):
    rows = P("seq", None)
    entry = P("seq", None, "tp")
    across = P("tp", "seq")
    along = P("seq", "tp")
    width = P(None, "seq")
    weights = (entry,) * 3 + (across,) * 3 + (along,) * 3 + (across,) * 3 + (across,) * 3 + (width,) * 3
    return jax.shard_map(
        per_device,
        mesh=mesh,
        in_specs=(rows, rows, P(), rows, rows, P("seq")) + weights,
        out_specs=(rows, rows) + weights,
        check_vma=False,
    )
```

```python
import functools
import math

import jax
import jax.numpy as jnp
from jax import lax
from jax.experimental import pallas as pl
from jax.experimental.pallas import tpu as pltpu
from jax.sharding import PartitionSpec as P

DH = 64
HASHES = 32
STEP = 10
LENGTH = 4096
QUERY_TILE = 256
KEY_TILE = 256
ROW_TILE = 256
WIDTH_LANE = 48
PLANES = 8

UNIT_EPS = 1e-06
NORM_EPS = 1e-05
BETA = 0.5
MATRIX_RATE = 0.02
VECTOR_RATE = 0.5
DECAY = 0.01
ADAM_EPS = 1e-08

f32 = jnp.float32
bf16 = jnp.bfloat16
i32 = jnp.int32


def dot_nt(a, b):
    return lax.dot_general(a, b, (((1,), (1,)), ((), ())), preferred_element_type=f32)


def dot_nn(a, b):
    return lax.dot_general(a, b, (((1,), (0,)), ((), ())), preferred_element_type=f32)


def dot_tn(a, b):
    return lax.dot_general(a, b, (((0,), (0,)), ((), ())), preferred_element_type=f32)


def kernel_call(kernel, outs, operands, scratch=(), smem=0, flops=10**9, name=None):
    spaces = [pltpu.SMEM] * smem + [pltpu.VMEM] * (len(operands) - smem)
    return pl.pallas_call(
        kernel,
        out_shape=[jax.ShapeDtypeStruct(shape, kind) for shape, kind in outs],
        in_specs=[pl.BlockSpec(memory_space=space) for space in spaces],
        out_specs=[pl.BlockSpec(memory_space=pltpu.VMEM)] * len(outs),
        scratch_shapes=list(scratch),
        compiler_params=pltpu.CompilerParams(vmem_limit_bytes=44 * 2**20),
        cost_estimate=pl.CostEstimate(
            flops=flops,
            bytes_accessed=sum(o.size * o.dtype.itemsize for o in operands),
            transcendentals=0,
        ),
        name=name,
    )(*operands)


def row_tiles(total):
    return [slice(r, r + ROW_TILE) for r in range(0, total, ROW_TILE)]


def left_half(rows):
    return lax.broadcasted_iota(i32, (rows, 2 * DH), 1) < DH


def half_sum(values, mask):
    return jnp.sum(jnp.where(mask, values, 0.0), axis=-1, keepdims=True)


def endings_of(len_ref):
    out = []
    total = jnp.int32(0)
    for s in range(len_ref.shape[0]):
        total = total + len_ref[s]
        out.append(total)
    return out


def labels_of(positions, ends):
    total = jnp.zeros(positions.shape, i32)
    for end in ends:
        total = total + (positions >= end).astype(i32)
    return total


def reach_of(first, last, ends):
    begin = jnp.int32(0)
    finish = jnp.int32(0)
    previous = jnp.int32(0)
    for end in ends:
        begin = jnp.where((first >= previous) & (first < end), previous, begin)
        finish = jnp.where((last >= previous) & (last < end), end, finish)
        previous = end
    return begin, finish


def pair_matches(wide, lane_planes, row_labels, lane_labels):
    parts = []
    for part in range(lane_planes.shape[1] // 128):
        lanes = slice(part * 128, part * 128 + 128)
        same = wide[0] ^ lane_planes[0:1, lanes]
        for b in range(1, PLANES):
            same = same & (wide[b] ^ lane_planes[b : b + 1, lanes])
        parts.append(same)
    matches = lax.population_count(jnp.concatenate(parts, axis=1))
    return jnp.where(row_labels == lane_labels, matches, 0).astype(f32)


def planes_of(codes):
    place = lax.broadcasted_iota(i32, codes.shape, 0)
    rows = []
    for b in range(PLANES):
        bits = ((codes >> b) & 1) << place
        part = bits[0:8] | bits[8:16] | bits[16:24] | bits[24:32]
        part = part | pltpu.roll(part, 4, 0)
        part = part | pltpu.roll(part, 2, 0)
        part = part | pltpu.roll(part, 1, 0)
        rows.append(part[0:1])
    return jnp.concatenate(rows, axis=0)


def block_planes(payload, rows, planes):
    width = payload.shape[1]
    for first in range(0, rows, width):
        place = rows + first // width * HASHES
        codes = payload[place : place + HASHES, :].astype(f32).astype(i32)
        size = min(width, rows - first)
        planes[:, first : first + size] = ~planes_of(codes[:, :size])


def placed(arrays):
    unique = []
    for array, _ in arrays:
        if not any(array is other for other in unique):
            unique.append(array)
    return unique, tuple(([array is other for other in unique].index(True), row) for array, row in arrays)


def attend_kernel(slots, places, len_ref, here_ref, query, own_planes, *refs):
    count = len(slots)
    arrays = 1 + max(index for index, _ in places)
    payloads = [refs[index].at[pl.ds(row, refs[index].shape[0] - row)] for index, row in places]
    refs = refs[arrays:]
    before = None
    if len(refs) == 4 + count:
        before, refs = refs[0], refs[1:]
    out, wide, total, planes = refs[0], refs[1], refs[2], refs[3:]
    block_rows, width = query.shape
    heads = width // 128
    ends = endings_of(len_ref)
    here = here_ref[0] * block_rows
    for (_, _, sent), payload, plane in zip(slots, payloads, planes):
        block_planes(payload, sent, plane)

    def own_tile(own, carry):
        rows = pl.ds(pl.multiple_of(own * QUERY_TILE, QUERY_TILE), QUERY_TILE)
        for b in range(PLANES):
            wide[b] = jnp.broadcast_to(own_planes[rows, b : b + 1], (QUERY_TILE, 128))
        total[...] = jnp.zeros_like(total)
        first = here + own * QUERY_TILE
        begin, finish = reach_of(first, first + (QUERY_TILE - 1), ends)
        row_labels = labels_of(first + lax.broadcasted_iota(i32, (QUERY_TILE, 1), 0), ends)
        for (offset, skipped, sent), keyval, plane in zip(slots, payloads, planes):
            start = here + offset * block_rows + skipped

            @pl.when((begin < start + sent) & (finish > start))
            def _(start=start, sent=sent, keyval=keyval, plane=plane):
                lane_labels = labels_of(start + lax.broadcasted_iota(i32, (1, sent), 1), ends)
                matches = pair_matches(wide, plane[...], row_labels, lane_labels)
                for h in range(heads):
                    lanes = slice(h * 128, h * 128 + 128)
                    pairs = keyval[:sent, lanes]
                    base = dot_nt(query[rows, lanes], pairs) + 1.0
                    base = base * base
                    base = base * base
                    total[:, lanes] += dot_nn((matches * (base * base)).astype(bf16), pairs)

        result = total[...] * (1.0 / (HASHES * 256.0))
        out[rows, :] = result if before is None else before[rows, :] + result
        return carry

    lax.fori_loop(0, block_rows // QUERY_TILE, own_tile, 0)


def back_kernel(slots, places, bundles, len_ref, here_ref, query, upstream, own_planes, *refs):
    count = len(slots)
    arrays = 1 + max(index for index, _ in places)
    payloads = [refs[index].at[pl.ds(row, refs[index].shape[0] - row)] for index, row in places]
    refs = refs[arrays:]
    before = None
    made = len(bundles)
    if len(refs) == 3 + made + count + 1:
        before, refs = refs[0], refs[1:]
    bundled, query_out, wide, total = refs[:made], refs[made], refs[made + 1], refs[made + 2]
    planes = refs[made + 3 :]
    outs = []
    for bundle, out in zip(bundles, bundled):
        filled = 0
        for sent in bundle:
            outs.append(out.at[pl.ds(filled, sent)])
            filled += sent
    block_rows, width = query.shape
    heads = width // 128
    ends = endings_of(len_ref)
    here = here_ref[0] * block_rows
    tiles = block_rows // QUERY_TILE
    query_out[...] = jnp.zeros_like(query_out) if before is None else before[...]
    for (_, _, sent), payload, plane in zip(slots, payloads, planes):
        block_planes(payload, sent, plane)
    for (offset, skipped, sent), keyval, plane, out in zip(slots, payloads, planes, outs):
        start = here + offset * block_rows + skipped
        begin, finish = reach_of(start, start + (sent - 1), ends)
        low = jnp.clip((begin - here) // QUERY_TILE, 0, tiles)
        high = jnp.clip((finish - here + (QUERY_TILE - 1)) // QUERY_TILE, 0, tiles)
        rows = slice(0, sent)
        total[:, rows, :] = jnp.zeros((2, sent, width), f32)

        @pl.when(low < high)
        def _(start=start, sent=sent, rows=rows, low=low, high=high, keyval=keyval, plane=plane):
            columns = jnp.transpose(plane[...])
            for b in range(PLANES):
                wide[b, rows] = jnp.broadcast_to(columns[:, b : b + 1], (sent, 128))
            row_labels = labels_of(start + lax.broadcasted_iota(i32, (sent, 1), 0), ends)

            def add_tile(tile, carry):
                place = pl.ds(pl.multiple_of(tile * QUERY_TILE, QUERY_TILE), QUERY_TILE)
                lane_labels = labels_of(
                    here + tile * QUERY_TILE + lax.broadcasted_iota(i32, (1, QUERY_TILE), 1), ends
                )
                matches = pair_matches(wide[:, rows], own_planes[:, place], row_labels, lane_labels)
                for h in range(heads):
                    lanes = slice(h * 128, h * 128 + 128)
                    pairs = keyval[rows, lanes]
                    asking = query[place, lanes]
                    arriving = upstream[place, lanes]
                    base = dot_nt(pairs, asking) + 1.0
                    grad = dot_nt(pairs, arriving)
                    square = base * base
                    power = matches * ((square * square) * (square * base))
                    grad_low = (grad * power).astype(bf16)
                    total[0, rows, lanes] += dot_nn(grad_low, asking)
                    total[1, rows, lanes] += dot_nn((power * base).astype(bf16), arriving)
                    query_out[place, lanes] += dot_tn(grad_low, pairs) * (4.0 / (HASHES * 128.0))
                return carry

            lax.fori_loop(low, high, add_tile, 0)

        out[...] = (
            total[0, rows] * (4.0 / (HASHES * 128.0)) + total[1, rows] * (1.0 / (HASHES * 256.0))
        ).astype(out.dtype)


def attend(slots, lengths, here, query, own_planes, payloads, before):
    block_rows, width = query.shape
    arrays, places = placed(payloads)
    operands = [lengths, here, query, own_planes, *arrays]
    if before is not None:
        operands.append(before)
    return kernel_call(
        functools.partial(attend_kernel, slots, places),
        [((block_rows, width), f32)],
        operands,
        scratch=[pltpu.VMEM((PLANES, QUERY_TILE, 128), i32), pltpu.VMEM((QUERY_TILE, width), f32)]
        + [pltpu.VMEM((PLANES, sent), i32) for _, _, sent in slots],
        smem=2,
        flops=sum(sent for _, _, sent in slots) * block_rows * 40000,
        name="attend",
    )[0]


def attend_back(sides, lengths, here, query, upstream, own_planes, near, before, weight=40000):
    block_rows, width = query.shape
    slots = tuple(slot for side in sides for slot in side)
    bundles = tuple(tuple(sent for _, _, sent in side) for side in sides)
    arrays, places = placed([near[offset] for offset, _, _ in slots])
    operands = [lengths, here, query, upstream, own_planes, *arrays]
    if before is not None:
        operands.append(before)
    *parts, total = kernel_call(
        functools.partial(back_kernel, slots, places, bundles),
        [((sum(bundle), width), bf16) for bundle in bundles] + [((block_rows, width), f32)],
        operands,
        scratch=[pltpu.VMEM((PLANES, block_rows, 128), i32), pltpu.VMEM((2, block_rows, width), f32)]
        + [pltpu.VMEM((PLANES, sent), i32) for _, _, sent in slots],
        smem=2,
        flops=sum(sent for _, _, sent in slots) * block_rows * weight,
        name="attend_back",
    )
    return parts, total


def combine_kernel(additions, own, *refs):
    sources, out = refs[:-1], refs[-1]
    out[...] = own[...]
    for source, (first, size, place) in zip(sources, additions):
        rows = slice(place, place + size)
        total = out[rows, :].astype(f32) + source[first : first + size, :].astype(f32)
        out[rows, :] = total.astype(bf16)


def combine(own, sources):
    return kernel_call(
        functools.partial(combine_kernel, tuple(place for _, place in sources)),
        [(own.shape, bf16)],
        [own] + [source for source, _ in sources],
        flops=10**8,
        name="combine",
    )[0]


def project_kernel(inputs, weights, bias, query_codes, key_codes, raw, query, payload, head, tail, lanes, columns):
    block_rows = inputs.shape[0]
    width = query.shape[1]
    heads = width // 128
    edge = head.shape[0] - HASHES
    left = left_half(ROW_TILE)
    for rows in row_tiles(block_rows):
        values = dot_nn(inputs[rows, :], weights[:, : 2 * width]) + bias[...]
        raw[rows, :] = values
        for h in range(heads):
            pair = values[:, h * 128 : h * 128 + 128]
            inverse = lax.rsqrt(half_sum(pair * pair, left) + UNIT_EPS)
            payload[rows, h * 128 : h * 128 + 128] = jnp.where(left, pair * inverse, pair).astype(bf16)
            asking = values[:, width + h * 128 : width + h * 128 + 128]
            inverse = lax.rsqrt(half_sum(asking * asking, left) + UNIT_EPS)
            query[rows, h * 128 : h * 128 + 128] = jnp.where(left, asking * inverse, 0.0).astype(bf16)
    codes = key_codes[...].astype(f32).astype(bf16)
    for first in range(0, block_rows, width):
        place = block_rows + first // width * HASHES
        payload[place : place + HASHES, :] = codes[:, first : first + width]
    head[0:edge, :] = payload[0:edge, :]
    tail[0:edge, :] = payload[block_rows - edge : block_rows, :]
    rest = jnp.zeros((HASHES, width - edge), bf16)
    head[edge:, :] = jnp.concatenate([codes[:, :edge], rest], axis=1)
    tail[edge:, :] = jnp.concatenate([codes[:, block_rows - edge :], rest], axis=1)
    planes = planes_of(query_codes[...])
    lanes[...] = planes
    for rows in row_tiles(block_rows):
        columns[rows, :] = jnp.transpose(planes[:, rows])


def mix_kernel(summed, weights, mixed, part):
    width = summed.shape[1]
    right = ~left_half(ROW_TILE)
    for rows in row_tiles(summed.shape[0]):
        for h in range(width // 128):
            lanes = slice(h * 128, h * 128 + 128)
            values = summed[rows, lanes]
            inverse = lax.rsqrt(half_sum(values * values, right) * (1.0 / DH) + NORM_EPS)
            mixed[rows, lanes] = jnp.where(right, values * inverse, 0.0).astype(bf16)
        part[rows, :] = dot_nt(mixed[rows, :], weights[:, width : 2 * width])


def row_mean(values):
    return jnp.sum(values, axis=-1, keepdims=True) * (1.0 / values.shape[-1])


def feed_kernel(inputs, attended, vectors, weights, bias, hidden, normed, inverse, active, slope, part):
    units = bias.shape[1]
    for rows in row_tiles(inputs.shape[0]):
        values = inputs[rows, :].astype(f32) + (attended[rows, :].astype(f32) + vectors[0:1, :])
        centre = values - row_mean(values)
        scale = lax.rsqrt(row_mean(centre * centre) + NORM_EPS)
        unit = centre * scale
        result = unit * vectors[2:3, :] + vectors[3:4, :]
        normed[rows, :] = unit
        inverse[rows, :] = scale
        hidden[rows, :] = result
        upper = dot_nn(result.astype(bf16), weights[:, :units]) + bias[...]
        curve = 0.5 * (1.0 + lax.erf(upper * math.sqrt(0.5)))
        active[rows, :] = (upper * curve).astype(bf16)
        slope[rows, :] = curve + upper * (jnp.exp(-0.5 * upper * upper) * (1.0 / math.sqrt(2.0 * math.pi)))
        part[rows, :] = dot_nt(active[rows, :], weights[:, units:])


def feed_back_kernel(hidden, fed, cotangent, scale, vectors, weights, active, slope, out, second, part, grads, width_sums, unit_sums, total):
    units = active.shape[1]
    total[...] = jnp.zeros_like(total)
    sums = [0.0, 0.0, 0.0]
    unit_sum = 0.0
    for rows in row_tiles(hidden.shape[0]):
        low = hidden[rows, :]
        values = low + (fed[rows, :].astype(f32) + vectors[1:2, :])
        centre = values - row_mean(values)
        inverse = lax.rsqrt(row_mean(centre * centre) + NORM_EPS)
        normed = centre * inverse
        out[rows, :] = (normed * vectors[4:5, :] + vectors[5:6, :]).astype(bf16)
        upstream = cotangent[rows, :].astype(f32) * scale[rows, :]
        sums[1] += jnp.sum(upstream * normed, axis=0, keepdims=True)
        sums[2] += jnp.sum(upstream, axis=0, keepdims=True)
        scaled = upstream * vectors[4:5, :]
        grad = inverse * (scaled - row_mean(scaled) - normed * row_mean(scaled * normed))
        second[rows, :] = grad
        grad_low = grad.astype(bf16)
        sums[0] += jnp.sum(grad_low.astype(f32), axis=0, keepdims=True)
        upper = (dot_nn(grad_low, weights[:, units:]) * slope[rows, :]).astype(bf16)
        unit_sum += jnp.sum(upper.astype(f32), axis=0, keepdims=True)
        part[rows, :] = dot_nt(upper, weights[:, :units])
        total[:, :units] += dot_tn(low.astype(bf16), upper)
        total[:, units:] += dot_tn(grad_low, active[rows, :])
    grads[...] = total[...].astype(bf16)
    width_sums[...] = jnp.concatenate(sums, axis=0)
    unit_sums[...] = unit_sum


def mix_back_kernel(second, came, normed, inverse, vectors, weights, mixed, summed, first, upstream, grads, width_sums, total):
    width = summed.shape[1]
    right = ~left_half(ROW_TILE)
    total[...] = jnp.zeros_like(total)
    sums = [0.0, 0.0, 0.0]
    for rows in row_tiles(second.shape[0]):
        hidden = second[rows, :] + came[rows, :].astype(f32)
        unit = normed[rows, :]
        sums[1] += jnp.sum(hidden * unit, axis=0, keepdims=True)
        sums[2] += jnp.sum(hidden, axis=0, keepdims=True)
        scaled = hidden * vectors[2:3, :]
        grad = inverse[rows, :] * (scaled - row_mean(scaled) - unit * row_mean(scaled * unit))
        first[rows, :] = grad
        grad_low = grad.astype(bf16)
        sums[0] += jnp.sum(grad_low.astype(f32), axis=0, keepdims=True)
        total[...] += dot_tn(grad_low, mixed[rows, :])
        arriving = dot_nn(grad_low, weights[:, width : 2 * width])
        for h in range(width // 128):
            lanes = slice(h * 128, h * 128 + 128)
            values = summed[rows, lanes]
            scale = lax.rsqrt(half_sum(values * values, right) * (1.0 / DH) + NORM_EPS)
            unit = values * scale
            piece = arriving[:, lanes]
            mean = half_sum(piece * unit, right) * (1.0 / DH)
            upstream[rows, lanes] = jnp.where(right, scale * (piece - unit * mean), 0.0).astype(bf16)
    grads[...] = total[...].astype(bf16)
    width_sums[...] = jnp.concatenate(sums, axis=0)


def project_back_kernel(count, ranks, inputs, weights, raw, query_grad, merge_grads, unit_sums, first_sums, second_sums, *refs):
    parts, (part, grads, total) = refs[:count], refs[count:]
    block_rows, width = query_grad.shape
    left = left_half(ROW_TILE)
    total[...] = jnp.zeros_like(total)
    column_sum = 0.0
    for rows in row_tiles(block_rows):
        pieces = []
        for h in range(width // 128):
            lanes = slice(h * 128, h * 128 + 128)
            came = 0.0
            for ref in parts:
                if ref.shape[0] == block_rows:
                    came = came + ref[rows, lanes].astype(f32)
            if rows.start == 0:
                came = came + parts[-2][:, lanes].astype(f32)
            if rows.stop == block_rows:
                came = came + parts[-1][:, lanes].astype(f32)
            values = raw[rows, lanes]
            scale = lax.rsqrt(half_sum(values * values, left) + UNIT_EPS)
            unit = values * scale
            along = half_sum(came * unit, left)
            pieces.append(jnp.where(left, scale * (came - unit * along), came).astype(bf16))
        for h in range(width // 128):
            lanes = slice(h * 128, h * 128 + 128)
            values = raw[rows, width + h * 128 : width + h * 128 + 128]
            scale = lax.rsqrt(half_sum(values * values, left) + UNIT_EPS)
            unit = values * scale
            came = query_grad[rows, lanes]
            along = half_sum(came * unit, left)
            pieces.append(jnp.where(left, scale * (came - unit * along), 0.0).astype(bf16))
        projected = jnp.concatenate(pieces, axis=1)
        column_sum += jnp.sum(projected.astype(f32), axis=0, keepdims=True)
        part[rows, :] = dot_nt(projected, weights[:, : 2 * width])
        total[...] += dot_tn(inputs[rows, :], projected)
    grads[:, :width] = total[:, :width].astype(bf16)
    grads[:, width : 2 * width] = (total[:, width:] + merge_grads[...].astype(f32)).astype(bf16)
    model_width = grads.shape[0]
    heads = width // (2 * DH)
    units = unit_sums.shape[1] // heads
    share = (3 * DH + units) // ranks
    spread = 0.0
    sources = [(column_sum, width + 2 * DH * h, 0, h, DH) for h in range(heads)]
    sources += [(column_sum, 2 * DH * h, DH, h, 2 * DH) for h in range(heads)]
    sources += [(unit_sums[...], units * h, 3 * DH, h, units) for h in range(heads)]
    for values, first, place, h, size in sources:
        size = size if size > DH else 2 * DH
        row = values[:, first : first + size]
        at = place + lax.broadcasted_iota(i32, (1, size), 1)
        if place == 0:
            row = jnp.where(at < DH, row, 0.0)
        owner = lax.broadcasted_iota(i32, (ranks, size), 0)
        picked = jnp.where((at >= owner * share) & (at < owner * share + share), row, 0.0)
        lane = lax.broadcasted_iota(i32, (size, 128), 1)
        source = place + lax.broadcasted_iota(i32, (size, 128), 0)
        moved = (lane - h * share == source % share) & (lane >= h * share) & (lane < h * share + share)
        spread = spread + dot_nn(picked.astype(bf16), moved.astype(f32).astype(bf16))
    rank_row = lax.broadcasted_iota(i32, (model_width, ranks), 0)
    rank = lax.broadcasted_iota(i32, (model_width, ranks), 1)
    where_to = (rank_row == rank * (model_width // ranks)).astype(f32).astype(bf16)
    width_sums = jnp.concatenate(
        [
            first_sums[0:1, :],
            second_sums[0:1, :],
            first_sums[1:3, :],
            second_sums[1:3, :],
            jnp.zeros((2, model_width), f32),
        ],
        axis=0,
    )
    lane = lax.broadcasted_iota(i32, (8, 128), 1)
    vector = lax.broadcasted_iota(i32, (8, 128), 0)
    vector_lane = ((lane == vector + WIDTH_LANE) & (vector < 6)).astype(f32).astype(bf16)
    grads[:, 2 * width :] = (
        dot_nn(where_to, spread.astype(bf16)) + dot_tn(width_sums.astype(bf16), vector_lane)
    ).astype(bf16)


def unpair(both):
    width = both.shape[1]
    first = [both[:, w : w + DH] for w in range(0, width, 2 * DH)]
    second = [both[:, w + DH : w + 2 * DH] for w in range(0, width, 2 * DH)]
    return jnp.concatenate(first, axis=1), jnp.concatenate(second, axis=1)


def update(grad, state, outs, rate, place=Ellipsis):
    weight, moment, square = (ref[place] for ref in state)
    moment_new = BETA * moment + (1.0 - BETA) * grad
    square_new = BETA * square + (1.0 - BETA) * grad * grad
    fix = 1.0 - BETA**STEP
    outs[0][place] = weight - rate * (
        moment_new * (1.0 / fix) / (jnp.sqrt(square_new * (1.0 / fix)) + ADAM_EPS) + DECAY * weight
    )
    outs[1][place] = moment_new
    outs[2][place] = square_new


def sum_of(parts):
    total = parts[0].astype(f32)
    for index in range(1, parts.shape[0]):
        total = total + parts[index].astype(f32)
    return total


def finish_first_kernel(parts, *refs):
    state, outs = refs[:12], refs[12:]
    total = sum_of(parts)
    width = state[3].shape[1]
    key, value = unpair(total[:, : 2 * width])
    query, merge = unpair(total[:, 2 * width : 4 * width])
    for which, grad in enumerate((query, key, value)):
        update(grad, state[0:3], outs[0:3], MATRIX_RATE, which)
    update(merge, state[3:6], outs[3:6], MATRIX_RATE)
    rest = total[:, 4 * width :]
    size = state[6].shape[1]
    for row in range(state[6].shape[0]):
        update(rest[0:1, row * size : row * size + size], state[6:9], outs[6:9], VECTOR_RATE, (slice(row, row + 1), slice(None)))
    update(jnp.transpose(rest)[WIDTH_LANE : WIDTH_LANE + 6, :], state[9:12], outs[9:12], VECTOR_RATE)


def finish_second_kernel(parts, *refs):
    state, outs = refs[:6], refs[6:]
    total = sum_of(parts)
    units = state[0].shape[1]
    update(total[:, :units], state[0:3], outs[0:3], MATRIX_RATE)
    update(total[:, units:], state[3:6], outs[3:6], MATRIX_RATE)


def shifted(value, steps):
    count = lax.axis_size("seq")
    return lax.ppermute(
        value, "seq", [(i, i + steps) for i in range(count) if 0 <= i + steps < count]
    )


def rotated(value, steps):
    count = lax.axis_size("seq")
    return lax.ppermute(value, "seq", [(i, (i + steps) % count) for i in range(count)])


def gather_rows(shard):
    count = lax.axis_size("seq")
    sent = jnp.broadcast_to(shard[None], (count,) + shard.shape)
    return lax.all_to_all(sent, "seq", 0, 0, tiled=True)


def scatter_rows(grads):
    count = lax.axis_size("seq")
    sent = grads.astype(bf16).reshape((count, grads.shape[0] // count) + grads.shape[1:])
    return lax.all_to_all(sent, "seq", 0, 0, tiled=True)


def swapped(value, mask):
    return lax.ppermute(value, "tp", [(i, i ^ mask) for i in range(lax.axis_size("tp"))])


def sum_over_tp(part):
    half = part.shape[0] // 2
    core = lax.axis_index("tp") % 2
    mine = lax.dynamic_slice_in_dim(part, core * half, half, 0)
    theirs = lax.dynamic_slice_in_dim(part, (1 - core) * half, half, 0).astype(bf16)
    here = (mine + swapped(theirs, 1).astype(f32)).astype(bf16)
    there = swapped(here, 2)
    total = (here.astype(f32) + there.astype(f32)).astype(bf16)
    other = swapped(total, 1)
    first = jnp.where(core == 0, total, other)
    second = jnp.where(core == 0, other, total)
    return jnp.concatenate([first, second], axis=0)


def paired(first, second):
    rows = first.shape[0]
    both = jnp.stack([first.reshape(rows, -1, DH), second.reshape(rows, -1, DH)], axis=2)
    return both.reshape(rows, -1)


def unpaired(both):
    rows = both.shape[0]
    split = both.reshape(rows, -1, 2, DH)
    return split[:, :, 0].reshape(rows, -1), split[:, :, 1].reshape(rows, -1)


def per_device(
    inputs,
    cotangent,
    lengths,
    query_codes,
    key_codes,
    masked,
    entry_weight,
    entry_moment,
    entry_square,
    merge_weight,
    merge_moment,
    merge_square,
    expand_weight,
    expand_moment,
    expand_square,
    reduce_weight,
    reduce_moment,
    reduce_square,
    split_bias,
    split_moment,
    split_square,
    width_params,
    width_moment,
    width_square,
):
    block_rows, model_width = inputs.shape
    count = lax.axis_size("seq")
    total_tokens = block_rows * count
    reach = (LENGTH - 2) // block_rows + 1
    heads = split_bias.shape[0]
    local = heads * DH
    shard_rows = model_width // count
    hidden_units = expand_weight.shape[1]
    split_columns = split_bias.shape[1]
    here_index = lax.axis_index("seq")
    here = here_index.astype(i32).reshape(1)

    masked_float = masked.astype(f32)
    masked_here = jnp.sum(masked)
    entry_shard = entry_weight.astype(bf16)
    split_flat = split_bias.astype(bf16).reshape(-1)
    split_pairs = jnp.pad(split_flat, (0, 2 * shard_rows - split_flat.shape[0]))
    counted = jnp.stack([masked_here // 256, masked_here % 256]).astype(bf16)
    extra = 4 * local
    first_shard = jnp.concatenate(
        [
            paired(entry_shard[:, 1], entry_shard[:, 2]),
            paired(entry_shard[:, 0], merge_weight.astype(bf16).T),
            width_params.astype(bf16).T,
            split_pairs.reshape(shard_rows, 2),
            jnp.pad(counted, (0, shard_rows - 2))[:, None],
            jnp.zeros((shard_rows, 119), bf16),
        ],
        axis=1,
    )
    first_full = gather_rows(first_shard)
    second_shard = jnp.concatenate(
        [expand_weight.astype(bf16), reduce_weight.astype(bf16).T], axis=1
    )
    weights = first_full.reshape(model_width, -1)
    vectors = first_full[:, :, extra : extra + 6].reshape(model_width, 6).T.astype(f32)
    split_float = (
        first_full[:, :, extra + 6 : extra + 8]
        .reshape(count, 2 * shard_rows)[:, : heads * split_columns]
        .reshape(count, heads, split_columns)
        .transpose(1, 0, 2)
        .reshape(heads, -1)
        .astype(f32)
    )
    masked_parts = first_full[:, :2, extra + 8].astype(f32)
    masked_total = jnp.sum(masked_parts[:, 0] * 256.0 + masked_parts[:, 1])
    scale = masked_float[:, None] * jnp.sqrt(total_tokens / (masked_total + 1.0))
    entry_bias = split_float[:, : 3 * DH].reshape(heads, 3, DH)
    entry_bias = jnp.concatenate(
        [
            paired(entry_bias[:, 1].reshape(1, -1), entry_bias[:, 2].reshape(1, -1)),
            paired(entry_bias[:, 0].reshape(1, -1), jnp.zeros((1, local), f32)),
        ],
        axis=1,
    )
    expand_bias = split_float[:, 3 * DH :].reshape(1, -1)

    far = KEY_TILE * -(-(LENGTH - 1 - (reach - 1) * block_rows) // KEY_TILE)
    slots = {0: (0, 0, block_rows)}
    for distance in range(1, reach):
        slots[distance] = (distance, 0, block_rows)
        slots[-distance] = (-distance, 0, block_rows)
    slots[reach] = (reach, 0, far)
    slots[-reach] = (-reach, block_rows - far, far)

    pair_width = 2 * local
    code_rows = HASHES * -(-block_rows // pair_width)
    raw, query, whole, head, tail, query_lanes, query_columns = kernel_call(
        project_kernel,
        [
            ((block_rows, 2 * pair_width), f32),
            ((block_rows, pair_width), bf16),
            ((block_rows + code_rows, pair_width), bf16),
            ((far + HASHES, pair_width), bf16),
            ((far + HASHES, pair_width), bf16),
            ((PLANES, block_rows), i32),
            ((block_rows, PLANES), i32),
        ],
        [inputs, weights, entry_bias, query_codes.T, key_codes.T],
        flops=6 * 10**9,
        name="project",
    )
    near = {0: (whole, 0), reach: (shifted(head, -reach), 0), -reach: (shifted(tail, reach), 0)}
    for side in (1, -1):
        near[side] = (rotated(whole, -side), 0)
        near[4 * side] = (rotated(whole, -4 * side), 0)
    both = jnp.concatenate([near[1][0], near[-1][0]], axis=0)
    for side in (1, -1):
        near[2 * side] = (rotated(near[side][0], -side), 0)
        got = rotated(both, -4 * side)
        near[4 * side + 1] = (got, 0)
        near[4 * side - 1] = (got, whole.shape[0])
    summed = None
    for offsets in ((0,), (1, -1, 4, -4, reach, -reach), (2, -2), (3, 5, -3, -5)):
        if offsets[0] == 2:
            second_shard, got = lax.optimization_barrier((second_shard, near[2][0]))
            near[2] = (got, 0)
            second_full = gather_rows(second_shard).reshape(model_width, -1)
        chosen = tuple(slots[o] for o in offsets)
        summed = attend(
            chosen, lengths, here, query, query_columns, [near[o] for o in offsets], summed
        )
    summed, second_full = lax.optimization_barrier((summed, second_full))

    square = (block_rows, model_width)
    mixed, part = kernel_call(
        mix_kernel,
        [((block_rows, pair_width), bf16), (square, f32)],
        [summed, weights],
        flops=3 * 10**9,
        name="mix",
    )
    attended = sum_over_tp(part)
    hidden, normed, inverse, active, slope, part = kernel_call(
        feed_kernel,
        [
            (square, f32),
            (square, f32),
            ((block_rows, 1), f32),
            ((block_rows, hidden_units), bf16),
            ((block_rows, hidden_units), f32),
            (square, f32),
        ],
        [inputs, attended, vectors, second_full, expand_bias],
        flops=8 * 10**9,
        name="feed",
    )
    fed = sum_over_tp(part)

    layer_out, grad_second, part, second_grads, second_sums, unit_sums = kernel_call(
        feed_back_kernel,
        [
            (square, bf16),
            (square, f32),
            (square, f32),
            ((model_width, 2 * hidden_units), bf16),
            ((3, model_width), f32),
            ((1, hidden_units), f32),
        ],
        [hidden, fed, cotangent, scale, vectors, second_full, active, slope],
        scratch=[pltpu.VMEM((model_width, 2 * hidden_units), f32)],
        flops=10 * 10**9,
        name="feed_back",
    )
    came = sum_over_tp(part)
    second_parts = scatter_rows(second_grads)
    grad_first, upstream, merge_grads, first_sums = kernel_call(
        mix_back_kernel,
        [
            (square, f32),
            ((block_rows, pair_width), bf16),
            ((model_width, pair_width), bf16),
            ((3, model_width), f32),
        ],
        [grad_second, came, normed, inverse, vectors, weights, mixed, summed],
        scratch=[pltpu.VMEM((model_width, pair_width), f32)],
        flops=6 * 10**9,
        name="mix_back",
    )
    def sides_of(*offsets):
        return [[slots[o] for o in side] for side in offsets]

    rest = (lengths, here, query, upstream, query_lanes, near)
    (right, left), grad_query = attend_back(sides_of((5, 3), (-5, -3)), *rest, None)
    far_right, far_left = rotated(right, 4), rotated(left, -4)
    (right, left, last_right, last_left), grad_query = attend_back(
        sides_of((2,), (-2,), (reach,), (-reach,)), *rest, grad_query
    )
    mid_right, mid_left = rotated(right, 1), rotated(left, -1)
    last_right, last_left = shifted(last_right, reach), shifted(last_left, -reach)
    (right, left, four_right, four_left), grad_query = attend_back(
        sides_of((1,), (-1,), (4,), (-4,)), *rest, grad_query, 1000
    )
    four_right, four_left = rotated(four_right, 4), rotated(four_left, -4)
    first, second = (0, block_rows, 0), (block_rows, block_rows, 0)
    right = combine(right, [(far_right, first), (far_left, second), (mid_right, first)])
    left = combine(left, [(far_left, first), (far_right, second), (mid_left, first)])
    next_right, next_left = rotated(right, 1), rotated(left, -1)
    (own,), grad_query = attend_back([[slots[0]]], *rest, grad_query)
    returned = [own, next_right, next_left, four_right, four_left, last_right, last_left]
    second_parts, grad_query = lax.optimization_barrier((second_parts, grad_query))
    part, first_grads = kernel_call(
        functools.partial(project_back_kernel, len(returned), count),
        [(square, f32), ((model_width, 2 * pair_width + 128), bf16)],
        [inputs, weights, raw, grad_query, merge_grads, unit_sums, first_sums, second_sums]
        + returned,
        scratch=[pltpu.VMEM((model_width, 2 * pair_width), f32)],
        flops=8 * 10**9,
        name="project_back",
    )
    input_sum = sum_over_tp(part)
    first_parts = scatter_rows(first_grads)
    second_parts, _ = lax.optimization_barrier((second_parts, first_grads))
    second_states = [
        expand_weight, expand_moment, expand_square, reduce_weight.T, reduce_moment.T, reduce_square.T,
    ]
    second_finished = kernel_call(
        finish_second_kernel,
        [(state.shape, f32) for state in second_states],
        [second_parts] + second_states,
        flops=10**8,
        name="finish_second",
    )
    input_grad = grad_first + input_sum.astype(f32)
    states = [
        entry_weight.transpose(1, 0, 2), entry_moment.transpose(1, 0, 2), entry_square.transpose(1, 0, 2),
        merge_weight.T, merge_moment.T, merge_square.T,
        split_bias, split_moment, split_square, width_params, width_moment, width_square,
    ]
    finished = kernel_call(
        finish_first_kernel,
        [(state.shape, f32) for state in states],
        [first_parts] + states,
        flops=10**8,
        name="finish_first",
    )
    return (
        layer_out,
        input_grad,
        *[array.transpose(1, 0, 2) for array in finished[:3]],
        *[array.T for array in finished[3:6]],
        *second_finished[:3],
        *[array.T for array in second_finished[3:]],
        *finished[6:],
    )


def solution(mesh):
    rows = P("seq", None)
    entry = P("seq", None, "tp")
    across = P("tp", "seq")
    along = P("seq", "tp")
    width = P(None, "seq")
    weights = (entry,) * 3 + (across,) * 3 + (along,) * 3 + (across,) * 3 + (across,) * 3 + (width,) * 3
    return jax.shard_map(
        per_device,
        mesh=mesh,
        in_specs=(rows, rows, P(), rows, rows, P("seq")) + weights,
        out_specs=(rows, rows) + weights,
        check_vma=False,
    )
```

```python
import functools
import math

import jax
import jax.numpy as jnp
from jax import lax
from jax.experimental import pallas as pl
from jax.experimental.pallas import tpu as pltpu
from jax.sharding import PartitionSpec as P

DH = 64
HASHES = 32
STEP = 10
LENGTH = 4096
QUERY_TILE = 256
KEY_TILE = 256
ROW_TILE = 256
WIDTH_LANE = 48
COUNT_LANE = 56
PLANES = 8

UNIT_EPS = 1e-06
NORM_EPS = 1e-05
BETA = 0.5
MATRIX_RATE = 0.02
VECTOR_RATE = 0.5
DECAY = 0.01
ADAM_EPS = 1e-08

f32 = jnp.float32
bf16 = jnp.bfloat16
i32 = jnp.int32


def dot_nt(a, b):
    return lax.dot_general(a, b, (((1,), (1,)), ((), ())), preferred_element_type=f32)


def dot_nn(a, b):
    return lax.dot_general(a, b, (((1,), (0,)), ((), ())), preferred_element_type=f32)


def dot_tn(a, b):
    return lax.dot_general(a, b, (((0,), (0,)), ((), ())), preferred_element_type=f32)


def kernel_call(kernel, outs, operands, scratch=(), smem=0, flops=10**9, name=None, vmem=24):
    spaces = [pltpu.SMEM] * smem + [pltpu.VMEM] * (len(operands) - smem)
    return pl.pallas_call(
        kernel,
        out_shape=[jax.ShapeDtypeStruct(shape, kind) for shape, kind in outs],
        in_specs=[pl.BlockSpec(memory_space=space) for space in spaces],
        out_specs=[pl.BlockSpec(memory_space=pltpu.VMEM)] * len(outs),
        scratch_shapes=list(scratch),
        compiler_params=pltpu.CompilerParams(vmem_limit_bytes=vmem * 2**20),
        cost_estimate=pl.CostEstimate(
            flops=flops,
            bytes_accessed=sum(o.size * o.dtype.itemsize for o in operands),
            transcendentals=0,
        ),
        name=name,
    )(*operands)


def row_tiles(total):
    return [slice(r, r + ROW_TILE) for r in range(0, total, ROW_TILE)]


def left_half(rows):
    return lax.broadcasted_iota(i32, (rows, 2 * DH), 1) < DH


def half_sum(values, mask):
    return jnp.sum(jnp.where(mask, values, 0.0), axis=-1, keepdims=True)


def endings_of(len_ref):
    out = []
    total = jnp.int32(0)
    for s in range(len_ref.shape[0]):
        total = total + len_ref[s]
        out.append(total)
    return out


def labels_of(positions, ends):
    total = jnp.zeros(positions.shape, i32)
    for end in ends:
        total = total + (positions >= end).astype(i32)
    return total


def reach_of(first, last, ends):
    begin = jnp.int32(0)
    finish = jnp.int32(0)
    previous = jnp.int32(0)
    for end in ends:
        begin = jnp.where((first >= previous) & (first < end), previous, begin)
        finish = jnp.where((last >= previous) & (last < end), end, finish)
        previous = end
    return begin, finish


def pair_matches(wide, lane_planes, row_labels, lane_labels):
    parts = []
    for part in range(lane_planes.shape[1] // 128):
        lanes = slice(part * 128, part * 128 + 128)
        same = wide[0] ^ lane_planes[0:1, lanes]
        for b in range(1, PLANES):
            same = same & (wide[b] ^ lane_planes[b : b + 1, lanes])
        parts.append(same)
    matches = lax.population_count(jnp.concatenate(parts, axis=1))
    return jnp.where(row_labels == lane_labels, matches, 0).astype(f32)


def planes_of(codes):
    place = lax.broadcasted_iota(i32, codes.shape, 0)
    rows = []
    for b in range(PLANES):
        bits = ((codes >> b) & 1) << place
        part = bits[0:8] | bits[8:16] | bits[16:24] | bits[24:32]
        part = part | pltpu.roll(part, 4, 0)
        part = part | pltpu.roll(part, 2, 0)
        part = part | pltpu.roll(part, 1, 0)
        rows.append(part[0:1])
    return jnp.concatenate(rows, axis=0)


def block_planes(payload, rows, planes):
    width = payload.shape[1]
    for first in range(0, rows, width):
        place = rows + first // width * HASHES
        codes = payload[place : place + HASHES, :].astype(f32).astype(i32)
        size = min(width, rows - first)
        planes[:, first : first + size] = ~planes_of(codes[:, :size])


def placed(arrays):
    unique = []
    for array, _ in arrays:
        if not any(array is other for other in unique):
            unique.append(array)
    return unique, tuple(([array is other for other in unique].index(True), row) for array, row in arrays)


def attend_kernel(slots, places, len_ref, here_ref, query, own_planes, *refs):
    count = len(slots)
    arrays = 1 + max(index for index, _ in places)
    payloads = [refs[index].at[pl.ds(row, refs[index].shape[0] - row)] for index, row in places]
    refs = refs[arrays:]
    before = None
    if len(refs) == 4 + count:
        before, refs = refs[0], refs[1:]
    out, wide, total, planes = refs[0], refs[1], refs[2], refs[3:]
    block_rows, width = query.shape
    heads = width // 128
    ends = endings_of(len_ref)
    here = here_ref[0] * block_rows
    for (_, _, sent), payload, plane in zip(slots, payloads, planes):
        block_planes(payload, sent, plane)

    def own_tile(own, carry):
        rows = pl.ds(pl.multiple_of(own * QUERY_TILE, QUERY_TILE), QUERY_TILE)
        for b in range(PLANES):
            wide[b] = jnp.broadcast_to(own_planes[rows, b : b + 1], (QUERY_TILE, 128))
        total[...] = jnp.zeros_like(total)
        first = here + own * QUERY_TILE
        begin, finish = reach_of(first, first + (QUERY_TILE - 1), ends)
        row_labels = labels_of(first + lax.broadcasted_iota(i32, (QUERY_TILE, 1), 0), ends)
        for (offset, skipped, sent), keyval, plane in zip(slots, payloads, planes):
            start = here + offset * block_rows + skipped

            @pl.when((begin < start + sent) & (finish > start))
            def _(start=start, sent=sent, keyval=keyval, plane=plane):
                lane_labels = labels_of(start + lax.broadcasted_iota(i32, (1, sent), 1), ends)
                matches = pair_matches(wide, plane[...], row_labels, lane_labels)
                for h in range(heads):
                    lanes = slice(h * 128, h * 128 + 128)
                    pairs = keyval[:sent, lanes]
                    base = dot_nt(query[rows, lanes], pairs) + 1.0
                    base = base * base
                    base = base * base
                    total[:, lanes] += dot_nn((matches * (base * base)).astype(bf16), pairs)

        result = total[...] * (1.0 / (HASHES * 256.0))
        out[rows, :] = result if before is None else before[rows, :] + result
        return carry

    lax.fori_loop(0, block_rows // QUERY_TILE, own_tile, 0)


def back_kernel(slots, places, bundles, len_ref, here_ref, query, upstream, own_planes, *refs):
    count = len(slots)
    arrays = 1 + max(index for index, _ in places)
    payloads = [refs[index].at[pl.ds(row, refs[index].shape[0] - row)] for index, row in places]
    refs = refs[arrays:]
    before = None
    made = len(bundles)
    if len(refs) == 3 + made + count + 1:
        before, refs = refs[0], refs[1:]
    bundled, query_out, wide, total = refs[:made], refs[made], refs[made + 1], refs[made + 2]
    planes = refs[made + 3 :]
    outs = []
    for bundle, out in zip(bundles, bundled):
        filled = 0
        for sent in bundle:
            outs.append(out.at[pl.ds(filled, sent)])
            filled += sent
    block_rows, width = query.shape
    heads = width // 128
    ends = endings_of(len_ref)
    here = here_ref[0] * block_rows
    tiles = block_rows // QUERY_TILE
    query_out[...] = jnp.zeros_like(query_out) if before is None else before[...]
    for (_, _, sent), payload, plane in zip(slots, payloads, planes):
        block_planes(payload, sent, plane)
    for (offset, skipped, sent), keyval, plane, out in zip(slots, payloads, planes, outs):
        start = here + offset * block_rows + skipped
        begin, finish = reach_of(start, start + (sent - 1), ends)
        low = jnp.clip((begin - here) // QUERY_TILE, 0, tiles)
        high = jnp.clip((finish - here + (QUERY_TILE - 1)) // QUERY_TILE, 0, tiles)
        rows = slice(0, sent)
        total[:, rows, :] = jnp.zeros((2, sent, width), f32)

        @pl.when(low < high)
        def _(start=start, sent=sent, rows=rows, low=low, high=high, keyval=keyval, plane=plane):
            columns = jnp.transpose(plane[...])
            for b in range(PLANES):
                wide[b, rows] = jnp.broadcast_to(columns[:, b : b + 1], (sent, 128))
            row_labels = labels_of(start + lax.broadcasted_iota(i32, (sent, 1), 0), ends)

            def add_tile(tile, carry):
                place = pl.ds(pl.multiple_of(tile * QUERY_TILE, QUERY_TILE), QUERY_TILE)
                lane_labels = labels_of(
                    here + tile * QUERY_TILE + lax.broadcasted_iota(i32, (1, QUERY_TILE), 1), ends
                )
                matches = pair_matches(wide[:, rows], own_planes[:, place], row_labels, lane_labels)
                for h in range(heads):
                    lanes = slice(h * 128, h * 128 + 128)
                    pairs = keyval[rows, lanes]
                    asking = query[place, lanes]
                    arriving = upstream[place, lanes]
                    base = dot_nt(pairs, asking) + 1.0
                    grad = dot_nt(pairs, arriving)
                    square = base * base
                    power = matches * ((square * square) * (square * base))
                    grad_low = (grad * power).astype(bf16)
                    total[0, rows, lanes] += dot_nn(grad_low, asking)
                    total[1, rows, lanes] += dot_nn((power * base).astype(bf16), arriving)
                    query_out[place, lanes] += dot_tn(grad_low, pairs) * (4.0 / (HASHES * 128.0))
                return carry

            lax.fori_loop(low, high, add_tile, 0)

        out[...] = (
            total[0, rows] * (4.0 / (HASHES * 128.0)) + total[1, rows] * (1.0 / (HASHES * 256.0))
        ).astype(out.dtype)


def attend(slots, lengths, here, query, own_planes, payloads, before, weight=40000):
    block_rows, width = query.shape
    arrays, places = placed(payloads)
    operands = [lengths, here, query, own_planes, *arrays]
    if before is not None:
        operands.append(before)
    return kernel_call(
        functools.partial(attend_kernel, slots, places),
        [((block_rows, width), f32)],
        operands,
        scratch=[pltpu.VMEM((PLANES, QUERY_TILE, 128), i32), pltpu.VMEM((QUERY_TILE, width), f32)]
        + [pltpu.VMEM((PLANES, sent), i32) for _, _, sent in slots],
        smem=2,
        flops=sum(sent for _, _, sent in slots) * block_rows * weight,
        name="attend",
    )[0]


def attend_back(sides, lengths, here, query, upstream, own_planes, near, before, weight=40000):
    block_rows, width = query.shape
    slots = tuple(slot for side in sides for slot in side)
    bundles = tuple(tuple(sent for _, _, sent in side) for side in sides)
    arrays, places = placed([near[offset] for offset, _, _ in slots])
    operands = [lengths, here, query, upstream, own_planes, *arrays]
    if before is not None:
        operands.append(before)
    *parts, total = kernel_call(
        functools.partial(back_kernel, slots, places, bundles),
        [((sum(bundle), width), bf16) for bundle in bundles] + [((block_rows, width), f32)],
        operands,
        scratch=[pltpu.VMEM((PLANES, block_rows, 128), i32), pltpu.VMEM((2, block_rows, width), f32)]
        + [pltpu.VMEM((PLANES, sent), i32) for _, _, sent in slots],
        smem=2,
        flops=sum(sent for _, _, sent in slots) * block_rows * weight,
        name="attend_back",
    )
    return parts, total


def combine_kernel(block_rows, right, left, far_right, far_left, mid_right, mid_left, to_right, to_left):
    first, second = slice(0, block_rows), slice(block_rows, 2 * block_rows)
    for own, far, across, mid, out in (
        (right, far_right, far_left, mid_right, to_right),
        (left, far_left, far_right, mid_left, to_left),
    ):
        total = own[...].astype(f32) + far[first, :].astype(f32)
        total = total + (across[second, :].astype(f32) + mid[...].astype(f32))
        out[...] = total.astype(bf16)


def unpack(parts, heads, share, entry_bias, expand_bias, vectors, scale, masked):
    ranks, rows, width = parts.shape
    extras = [parts[rank, :, width - 128 :].astype(f32) for rank in range(ranks)]
    firsts = jnp.concatenate([extra[0:1, :] for extra in extras], axis=0).astype(bf16)
    total = ranks * share
    units = total - 3 * DH
    for h in range(heads):
        lane = lax.broadcasted_iota(i32, (128, total), 0)
        place = lax.broadcasted_iota(i32, (128, total), 1)
        moved = (lane == h * share + place % share).astype(f32).astype(bf16)
        spread = dot_nn(firsts, moved)
        owner = lax.broadcasted_iota(i32, (ranks, total), 0)
        at = lax.broadcasted_iota(i32, (ranks, total), 1)
        owned = (at >= owner * share) & (at < owner * share + share)
        biases = jnp.sum(jnp.where(owned, spread, 0.0), axis=0, keepdims=True)
        zeros = jnp.zeros((1, DH), f32)
        half = heads * 2 * DH
        entry_bias[:, h * 2 * DH : h * 2 * DH + 2 * DH] = biases[:, DH : 3 * DH]
        entry_bias[:, half + h * 2 * DH : half + h * 2 * DH + 2 * DH] = jnp.concatenate(
            [biases[:, :DH], zeros], axis=1
        )
        expand_bias[:, h * units : h * units + units] = biases[:, 3 * DH :]
    place = lax.broadcasted_iota(i32, (8, 128), 1) == lax.broadcasted_iota(i32, (8, 128), 0) + WIDTH_LANE
    vectors[...] = dot_nt(
        place.astype(f32).astype(bf16), jnp.concatenate(extras, axis=0).astype(bf16)
    )
    lane = lax.broadcasted_iota(i32, (ranks, 128), 1)
    counts = firsts.astype(f32)
    marked = jnp.where(lane == COUNT_LANE, 256.0 * counts, jnp.where(lane == COUNT_LANE + 1, counts, 0.0))
    marked = jnp.sum(jnp.sum(marked, axis=1, keepdims=True), axis=0, keepdims=True)
    tokens = masked.shape[0] * ranks
    scale[...] = masked[...].astype(f32) * jnp.sqrt(tokens / (marked + 1.0))


def project_kernel(
    heads, share, inputs, parts, query_codes, key_codes, masked,
    raw, query, payload, head, tail, lanes, columns, expand_bias, vectors, scale, weights_out, bias,
):
    unpack(parts, heads, share, bias, expand_bias, vectors, scale, masked)
    shard = parts.shape[1]
    for rank in range(0, parts.shape[0], 2):
        both = jnp.concatenate([parts[rank].astype(f32), parts[rank + 1].astype(f32)], axis=0)
        weights_out[rank * shard : (rank + 2) * shard, :] = both.astype(bf16)
    weights = weights_out
    block_rows = inputs.shape[0]
    width = query.shape[1]
    heads = width // 128
    edge = head.shape[0] - HASHES
    left = left_half(ROW_TILE)
    for rows in row_tiles(block_rows):
        values = dot_nn(inputs[rows, :], weights[:, : 2 * width]) + bias[...]
        raw[rows, :] = values
        for h in range(heads):
            pair = values[:, h * 128 : h * 128 + 128]
            inverse = lax.rsqrt(half_sum(pair * pair, left) + UNIT_EPS)
            payload[rows, h * 128 : h * 128 + 128] = jnp.where(left, pair * inverse, pair).astype(bf16)
            asking = values[:, width + h * 128 : width + h * 128 + 128]
            inverse = lax.rsqrt(half_sum(asking * asking, left) + UNIT_EPS)
            query[rows, h * 128 : h * 128 + 128] = jnp.where(left, asking * inverse, 0.0).astype(bf16)
    codes = key_codes[...].astype(f32).astype(bf16)
    for first in range(0, block_rows, width):
        place = block_rows + first // width * HASHES
        payload[place : place + HASHES, :] = codes[:, first : first + width]
    head[0:edge, :] = payload[0:edge, :]
    tail[0:edge, :] = payload[block_rows - edge : block_rows, :]
    rest = jnp.zeros((HASHES, width - edge), bf16)
    head[edge:, :] = jnp.concatenate([codes[:, :edge], rest], axis=1)
    tail[edge:, :] = jnp.concatenate([codes[:, block_rows - edge :], rest], axis=1)
    planes = planes_of(query_codes[...])
    lanes[...] = planes
    for rows in row_tiles(block_rows):
        columns[rows, :] = jnp.transpose(planes[:, rows])


def halve(core_ref, whole, mine, theirs):
    half = mine.shape[0]
    first = pl.multiple_of(core_ref[0] * half, half)
    mine[...] = whole[pl.ds(first, half), :]
    theirs[...] = whole[pl.ds(half - first, half), :].astype(bf16)


def unite(core_ref, mine, other, whole):
    half = mine.shape[0]
    first = pl.multiple_of(core_ref[0] * half, half)
    whole[pl.ds(first, half), :] = mine[...]
    whole[pl.ds(half - first, half), :] = other[...]


def mix_kernel(core, summed, weights, mixed, mine, theirs, part):
    width = summed.shape[1]
    right = ~left_half(ROW_TILE)
    for rows in row_tiles(summed.shape[0]):
        for h in range(width // 128):
            lanes = slice(h * 128, h * 128 + 128)
            values = summed[rows, lanes]
            inverse = lax.rsqrt(half_sum(values * values, right) * (1.0 / DH) + NORM_EPS)
            mixed[rows, lanes] = jnp.where(right, values * inverse, 0.0).astype(bf16)
        part[rows, :] = dot_nt(mixed[rows, :], weights[:, width : 2 * width])
    halve(core, part, mine, theirs)


def row_mean(values):
    return jnp.sum(values, axis=-1, keepdims=True) * (1.0 / values.shape[-1])


def feed_kernel(
    core, inputs, total, other, vectors, weights, bias, hidden, normed, inverse, active, slope, mine, theirs, attended, part
):
    units = bias.shape[1]
    unite(core, total, other, attended)
    for rows in row_tiles(inputs.shape[0]):
        values = inputs[rows, :].astype(f32) + (attended[rows, :].astype(f32) + vectors[0:1, :])
        centre = values - row_mean(values)
        scale = lax.rsqrt(row_mean(centre * centre) + NORM_EPS)
        unit = centre * scale
        result = unit * vectors[2:3, :] + vectors[3:4, :]
        normed[rows, :] = unit.astype(bf16)
        inverse[rows, :] = scale
        hidden[rows, :] = result
        upper = dot_nn(result.astype(bf16), weights[:, :units]) + bias[...]
        curve = 0.5 * (1.0 + lax.erf(upper * math.sqrt(0.5)))
        active[rows, :] = (upper * curve).astype(bf16)
        slope[rows, :] = (
            curve + upper * (jnp.exp(-0.5 * upper * upper) * (1.0 / math.sqrt(2.0 * math.pi)))
        ).astype(bf16)
        part[rows, :] = dot_nt(active[rows, :], weights[:, units:])
    halve(core, part, mine, theirs)


def feed_back_kernel(
    core, hidden, fed_mine, fed_other, cotangent, scale, vectors, weights, active, slope,
    out, second, mine, theirs, grads, width_sums, unit_sums, total, fed, part,
):
    units = active.shape[1]
    unite(core, fed_mine, fed_other, fed)
    total[...] = jnp.zeros_like(total)
    sums = [0.0, 0.0, 0.0]
    unit_sum = 0.0
    for rows in row_tiles(hidden.shape[0]):
        low = hidden[rows, :]
        values = low + (fed[rows, :].astype(f32) + vectors[1:2, :])
        centre = values - row_mean(values)
        inverse = lax.rsqrt(row_mean(centre * centre) + NORM_EPS)
        normed = centre * inverse
        out[rows, :] = (normed * vectors[4:5, :] + vectors[5:6, :]).astype(bf16)
        upstream = cotangent[rows, :].astype(f32) * scale[rows, :]
        sums[1] += jnp.sum(upstream * normed, axis=0, keepdims=True)
        sums[2] += jnp.sum(upstream, axis=0, keepdims=True)
        scaled = upstream * vectors[4:5, :]
        grad = inverse * (scaled - row_mean(scaled) - normed * row_mean(scaled * normed))
        second[rows, :] = grad
        grad_low = grad.astype(bf16)
        sums[0] += jnp.sum(grad_low.astype(f32), axis=0, keepdims=True)
        upper = (dot_nn(grad_low, weights[:, units:]) * slope[rows, :].astype(f32)).astype(bf16)
        unit_sum += jnp.sum(upper.astype(f32), axis=0, keepdims=True)
        part[rows, :] = dot_nt(upper, weights[:, :units])
        total[:, :units] += dot_tn(low.astype(bf16), upper)
        total[:, units:] += dot_tn(grad_low, active[rows, :])
    halve(core, part, mine, theirs)
    grads[...] = total[...].astype(bf16)
    width_sums[...] = jnp.concatenate(sums, axis=0)
    unit_sums[...] = unit_sum


def mix_back_kernel(core, second, came_mine, came_other, normed, inverse, vectors, weights, mixed, summed, first, upstream, grads, width_sums, total, came):
    width = summed.shape[1]
    unite(core, came_mine, came_other, came)
    right = ~left_half(ROW_TILE)
    total[...] = jnp.zeros_like(total)
    sums = [0.0, 0.0, 0.0]
    for rows in row_tiles(second.shape[0]):
        hidden = second[rows, :] + came[rows, :].astype(f32)
        unit = normed[rows, :].astype(f32)
        sums[1] += jnp.sum(hidden * unit, axis=0, keepdims=True)
        sums[2] += jnp.sum(hidden, axis=0, keepdims=True)
        scaled = hidden * vectors[2:3, :]
        grad = inverse[rows, :] * (scaled - row_mean(scaled) - unit * row_mean(scaled * unit))
        first[rows, :] = grad
        grad_low = grad.astype(bf16)
        sums[0] += jnp.sum(grad_low.astype(f32), axis=0, keepdims=True)
        total[...] += dot_tn(grad_low, mixed[rows, :])
        arriving = dot_nn(grad_low, weights[:, width : 2 * width])
        for h in range(width // 128):
            lanes = slice(h * 128, h * 128 + 128)
            values = summed[rows, lanes]
            scale = lax.rsqrt(half_sum(values * values, right) * (1.0 / DH) + NORM_EPS)
            unit = values * scale
            piece = arriving[:, lanes]
            mean = half_sum(piece * unit, right) * (1.0 / DH)
            upstream[rows, lanes] = jnp.where(right, scale * (piece - unit * mean), 0.0).astype(bf16)
    grads[...] = total[...].astype(bf16)
    width_sums[...] = jnp.concatenate(sums, axis=0)


def project_back_kernel(count, ranks, core, inputs, weights, raw, query_grad, merge_grads, unit_sums, first_sums, second_sums, *refs):
    parts, (mine, theirs, grads, total, part) = refs[:count], refs[count:]
    block_rows, width = query_grad.shape
    left = left_half(ROW_TILE)
    total[...] = jnp.zeros_like(total)
    column_sum = 0.0
    for rows in row_tiles(block_rows):
        pieces = []
        for h in range(width // 128):
            lanes = slice(h * 128, h * 128 + 128)
            came = 0.0
            for ref in parts:
                if ref.shape[0] == block_rows:
                    came = came + ref[rows, lanes].astype(f32)
            if rows.start == 0:
                came = came + parts[-2][:, lanes].astype(f32)
            if rows.stop == block_rows:
                came = came + parts[-1][:, lanes].astype(f32)
            values = raw[rows, lanes]
            scale = lax.rsqrt(half_sum(values * values, left) + UNIT_EPS)
            unit = values * scale
            along = half_sum(came * unit, left)
            pieces.append(jnp.where(left, scale * (came - unit * along), came).astype(bf16))
        for h in range(width // 128):
            lanes = slice(h * 128, h * 128 + 128)
            values = raw[rows, width + h * 128 : width + h * 128 + 128]
            scale = lax.rsqrt(half_sum(values * values, left) + UNIT_EPS)
            unit = values * scale
            came = query_grad[rows, lanes]
            along = half_sum(came * unit, left)
            pieces.append(jnp.where(left, scale * (came - unit * along), 0.0).astype(bf16))
        projected = jnp.concatenate(pieces, axis=1)
        column_sum += jnp.sum(projected.astype(f32), axis=0, keepdims=True)
        part[rows, :] = dot_nt(projected, weights[:, : 2 * width])
        total[...] += dot_tn(inputs[rows, :], projected)
    grads[:, :width] = total[:, :width].astype(bf16)
    grads[:, width : 2 * width] = (total[:, width:] + merge_grads[...].astype(f32)).astype(bf16)
    halve(core, part, mine, theirs)
    model_width = grads.shape[0]
    heads = width // (2 * DH)
    units = unit_sums.shape[1] // heads
    share = (3 * DH + units) // ranks
    spread = 0.0
    sources = [(column_sum, width + 2 * DH * h, 0, h, DH) for h in range(heads)]
    sources += [(column_sum, 2 * DH * h, DH, h, 2 * DH) for h in range(heads)]
    sources += [(unit_sums[...], units * h, 3 * DH, h, units) for h in range(heads)]
    for values, first, place, h, size in sources:
        size = size if size > DH else 2 * DH
        row = values[:, first : first + size]
        at = place + lax.broadcasted_iota(i32, (1, size), 1)
        if place == 0:
            row = jnp.where(at < DH, row, 0.0)
        owner = lax.broadcasted_iota(i32, (ranks, size), 0)
        picked = jnp.where((at >= owner * share) & (at < owner * share + share), row, 0.0)
        lane = lax.broadcasted_iota(i32, (size, 128), 1)
        source = place + lax.broadcasted_iota(i32, (size, 128), 0)
        moved = (lane - h * share == source % share) & (lane >= h * share) & (lane < h * share + share)
        spread = spread + dot_nn(picked.astype(bf16), moved.astype(f32).astype(bf16))
    rank_row = lax.broadcasted_iota(i32, (model_width, ranks), 0)
    rank = lax.broadcasted_iota(i32, (model_width, ranks), 1)
    where_to = (rank_row == rank * (model_width // ranks)).astype(f32).astype(bf16)
    width_sums = jnp.concatenate(
        [
            first_sums[0:1, :],
            second_sums[0:1, :],
            first_sums[1:3, :],
            second_sums[1:3, :],
            jnp.zeros((2, model_width), f32),
        ],
        axis=0,
    )
    lane = lax.broadcasted_iota(i32, (8, 128), 1)
    vector = lax.broadcasted_iota(i32, (8, 128), 0)
    vector_lane = ((lane == vector + WIDTH_LANE) & (vector < 6)).astype(f32).astype(bf16)
    grads[:, 2 * width :] = (
        dot_nn(where_to, spread.astype(bf16)) + dot_tn(width_sums.astype(bf16), vector_lane)
    ).astype(bf16)


def unpair(both):
    width = both.shape[1]
    first = [both[:, w : w + DH] for w in range(0, width, 2 * DH)]
    second = [both[:, w + DH : w + 2 * DH] for w in range(0, width, 2 * DH)]
    return jnp.concatenate(first, axis=1), jnp.concatenate(second, axis=1)


def update(grad, state, outs, rate, place=Ellipsis):
    weight, moment, square = (ref[place] for ref in state)
    moment_new = BETA * moment + (1.0 - BETA) * grad
    square_new = BETA * square + (1.0 - BETA) * grad * grad
    fix = 1.0 - BETA**STEP
    outs[0][place] = weight - rate * (
        moment_new * (1.0 / fix) / (jnp.sqrt(square_new * (1.0 / fix)) + ADAM_EPS) + DECAY * weight
    )
    outs[1][place] = moment_new
    outs[2][place] = square_new


def sum_of(parts):
    total = parts[0].astype(f32)
    for index in range(1, parts.shape[0]):
        total = total + parts[index].astype(f32)
    return total


def finish_first_kernel(parts, *refs):
    state, outs = refs[:12], refs[12:]
    total = sum_of(parts)
    width = state[3].shape[1]
    key, value = unpair(total[:, : 2 * width])
    query, merge = unpair(total[:, 2 * width : 4 * width])
    for which, grad in enumerate((query, key, value)):
        update(grad, state[0:3], outs[0:3], MATRIX_RATE, which)
    update(merge, state[3:6], outs[3:6], MATRIX_RATE)
    rest = total[:, 4 * width :]
    size = state[6].shape[1]
    for row in range(state[6].shape[0]):
        update(rest[0:1, row * size : row * size + size], state[6:9], outs[6:9], VECTOR_RATE, (slice(row, row + 1), slice(None)))
    update(jnp.transpose(rest)[WIDTH_LANE : WIDTH_LANE + 6, :], state[9:12], outs[9:12], VECTOR_RATE)


def finish_second_kernel(parts, *refs):
    state, outs = refs[:6], refs[6:]
    total = sum_of(parts)
    units = state[0].shape[1]
    update(total[:, :units], state[0:3], outs[0:3], MATRIX_RATE)
    update(total[:, units:], state[3:6], outs[3:6], MATRIX_RATE)


def pack_kernel(entry, merge, width, split, masked, expand, reduce, out, later):
    rows = entry.shape[1]
    pieces = []
    for first, second in ((entry[1], entry[2]), (entry[0], merge[...])):
        for h in range(0, entry.shape[2], DH):
            pieces += [first[:, h : h + DH], second[:, h : h + DH]]
    heads, size = split.shape
    lane = lax.broadcasted_iota(i32, (size, 128), 1)
    index = lax.broadcasted_iota(i32, (size, 128), 0)
    biases = 0.0
    for h in range(heads):
        moved = (lane == index + h * size).astype(f32).astype(bf16)
        biases = biases + dot_nn(split[h : h + 1, :].astype(bf16), moved)
    marked = jnp.sum(jnp.sum(masked[...].astype(f32), axis=1, keepdims=True), axis=0, keepdims=True)
    high = jnp.floor(marked * (1.0 / 256.0))
    lane = lax.broadcasted_iota(i32, (1, 128), 1)
    biases = biases + jnp.where(lane == COUNT_LANE, high, 0.0)
    biases = biases + jnp.where(lane == COUNT_LANE + 1, marked - 256.0 * high, 0.0)
    place = (
        lax.broadcasted_iota(i32, (6, 128), 1) == lax.broadcasted_iota(i32, (6, 128), 0) + WIDTH_LANE
    )
    vectors = dot_tn(width[...].astype(bf16), place.astype(f32).astype(bf16))
    first_row = lax.broadcasted_iota(i32, (rows, 128), 0) == 0
    pieces.append(vectors + jnp.where(first_row, biases, 0.0))
    packed = jnp.concatenate(pieces, axis=1).astype(bf16)
    rest = jnp.concatenate([expand[...].astype(bf16), reduce[...].astype(bf16)], axis=1)
    for rank in range(out.shape[0]):
        out[rank] = packed
        later[rank] = rest


def shifted(value, steps):
    count = lax.axis_size("seq")
    return lax.ppermute(
        value, "seq", [(i, i + steps) for i in range(count) if 0 <= i + steps < count]
    )


def rotated(value, steps):
    count = lax.axis_size("seq")
    return lax.ppermute(value, "seq", [(i, (i + steps) % count) for i in range(count)])


def scatter_rows(grads):
    count = lax.axis_size("seq")
    sent = grads.astype(bf16).reshape((count, grads.shape[0] // count) + grads.shape[1:])
    return lax.all_to_all(sent, "seq", 0, 0, tiled=True)


def swapped(value, mask):
    return lax.ppermute(value, "tp", [(i, i ^ mask) for i in range(lax.axis_size("tp"))])


def sum_over_tp(mine, theirs):
    here = (mine + swapped(theirs, 1).astype(f32)).astype(bf16)
    there = swapped(here, 2)
    total = (here.astype(f32) + there.astype(f32)).astype(bf16)
    return total, swapped(total, 1)


def per_device(
    inputs,
    cotangent,
    lengths,
    query_codes,
    key_codes,
    masked,
    entry_weight,
    entry_moment,
    entry_square,
    merge_weight,
    merge_moment,
    merge_square,
    expand_weight,
    expand_moment,
    expand_square,
    reduce_weight,
    reduce_moment,
    reduce_square,
    split_bias,
    split_moment,
    split_square,
    width_params,
    width_moment,
    width_square,
):
    block_rows, model_width = inputs.shape
    count = lax.axis_size("seq")
    total_tokens = block_rows * count
    reach = (LENGTH - 2) // block_rows + 1
    heads = split_bias.shape[0]
    local = heads * DH
    shard_rows = model_width // count
    hidden_units = expand_weight.shape[1]
    split_columns = split_bias.shape[1]
    here_index = lax.axis_index("seq")
    here = here_index.astype(i32).reshape(1)

    extra = 4 * local
    first_shards, second_shards = kernel_call(
        pack_kernel,
        [((count, shard_rows, extra + 128), bf16), ((count, shard_rows, 2 * hidden_units), bf16)],
        [
            entry_weight.transpose(1, 0, 2), merge_weight.T, width_params, split_bias,
            masked.reshape(-1, 128), expand_weight, reduce_weight.T,
        ],
        flops=10**8,
        name="pack",
    )
    first_full = lax.all_to_all(first_shards, "seq", 0, 0, tiled=True)
    far = KEY_TILE * -(-(LENGTH - 1 - (reach - 1) * block_rows) // KEY_TILE)
    slots = {0: (0, 0, block_rows)}
    for distance in range(1, reach):
        slots[distance] = (distance, 0, block_rows)
        slots[-distance] = (-distance, 0, block_rows)
    slots[reach] = (reach, 0, far)
    slots[-reach] = (-reach, block_rows - far, far)

    pair_width = 2 * local
    code_rows = HASHES * -(-block_rows // pair_width)
    (
        raw, query, whole, head, tail, query_lanes, query_columns, expand_bias, vectors, scale, weights
    ) = kernel_call(
        functools.partial(project_kernel, heads, split_columns),
        [
            ((block_rows, 2 * pair_width), f32),
            ((block_rows, pair_width), bf16),
            ((block_rows + code_rows, pair_width), bf16),
            ((far + HASHES, pair_width), bf16),
            ((far + HASHES, pair_width), bf16),
            ((PLANES, block_rows), i32),
            ((block_rows, PLANES), i32),
            ((1, hidden_units), f32),
            ((8, model_width), f32),
            ((block_rows, 1), f32),
            ((model_width, extra + 128), bf16),
        ],
        [inputs, first_full, query_codes.T, key_codes.T, masked.reshape(-1, 1)],
        scratch=[pltpu.VMEM((1, 2 * pair_width), f32)],
        flops=10**9,
        name="project",
    )
    near = {0: (whole, 0)}
    for side in (1, -1):
        near[side] = (rotated(whole, -side), 0)
        near[4 * side] = (rotated(whole, -4 * side), 0)
    both = jnp.concatenate([near[1][0], near[-1][0]], axis=0)
    for side in (1, -1):
        near[2 * side] = (rotated(near[side][0], -side), 0)
        got = rotated(both, -4 * side)
        near[4 * side + 1] = (got, 0)
        near[4 * side - 1] = (got, whole.shape[0])
    summed = None
    for offsets in ((0,), (1, -1, 4, -4), (2, -2), (3, 5, -3, -5, reach, -reach)):
        if offsets[0] == 2:
            second_shards, got = lax.optimization_barrier((second_shards, near[2][0]))
            near[2] = (got, 0)
            second_full = lax.all_to_all(second_shards, "seq", 0, 0, tiled=True)
            second_full = second_full.reshape(model_width, -1)
        chosen = tuple(slots[o] for o in offsets)
        summed = attend(
            chosen, lengths, here, query, query_columns, [near[o] for o in offsets], summed,
        )
        if offsets[0] == 1:
            head, tail, summed = lax.optimization_barrier((head, tail, summed))
            near[reach], near[-reach] = (shifted(head, -reach), 0), (shifted(tail, reach), 0)

    summed, second_full = lax.optimization_barrier((summed, second_full))

    square = (block_rows, model_width)
    halves = [((block_rows // 2, model_width), f32), ((block_rows // 2, model_width), bf16)]
    core = (lax.axis_index("tp") % 2).astype(i32).reshape(1)
    united = pltpu.VMEM(square, bf16)
    partial = pltpu.VMEM(square, f32)
    mixed, *parts = kernel_call(
        mix_kernel,
        [((block_rows, pair_width), bf16)] + halves,
        [core, summed, weights],
        scratch=[partial],
        smem=1,
        flops=3 * 10**9,
        name="mix",
    )
    attended = sum_over_tp(*parts)
    hidden, normed, inverse, active, slope, *parts = kernel_call(
        feed_kernel,
        [
            (square, f32),
            (square, bf16),
            ((block_rows, 1), f32),
            ((block_rows, hidden_units), bf16),
            ((block_rows, hidden_units), bf16),
        ]
        + halves,
        [core, inputs, *attended, vectors, second_full, expand_bias],
        scratch=[united, partial],
        smem=1,
        flops=8 * 10**9,
        name="feed",
    )
    fed = sum_over_tp(*parts)

    layer_out, grad_second, *parts, second_grads, second_sums, unit_sums = kernel_call(
        feed_back_kernel,
        [
            (square, bf16),
            (square, f32),
            *halves,
            ((model_width, 2 * hidden_units), bf16),
            ((3, model_width), f32),
            ((1, hidden_units), f32),
        ],
        [core, hidden, *fed, cotangent, scale, vectors, second_full, active, slope],
        scratch=[pltpu.VMEM((model_width, 2 * hidden_units), f32), united, partial],
        smem=1,
        flops=10 * 10**9,
        name="feed_back",
    )
    came = sum_over_tp(*parts)
    second_parts = scatter_rows(second_grads)
    grad_first, upstream, merge_grads, first_sums = kernel_call(
        mix_back_kernel,
        [
            (square, f32),
            ((block_rows, pair_width), bf16),
            ((model_width, pair_width), bf16),
            ((3, model_width), f32),
        ],
        [core, grad_second, *came, normed, inverse, vectors, weights, mixed, summed],
        scratch=[pltpu.VMEM((model_width, pair_width), f32), united],
        smem=1,
        flops=6 * 10**9,
        name="mix_back",
    )
    def sides_of(*offsets):
        return [[slots[o] for o in side] for side in offsets]

    rest = (lengths, here, query, upstream, query_lanes, near)
    (right, left), grad_query = attend_back(sides_of((5, 3), (-5, -3)), *rest, None)
    far_right, far_left = rotated(right, 4), rotated(left, -4)
    second_parts, grad_query = lax.optimization_barrier((second_parts, grad_query))
    (right, left, last_right, last_left), grad_query = attend_back(
        sides_of((2,), (-2,), (reach,), (-reach,)), *rest, grad_query
    )
    mid_right, mid_left = rotated(right, 1), rotated(left, -1)
    last_right, last_left = rotated(last_right, reach), rotated(last_left, -reach)
    (right, left, four_right, four_left), grad_query = attend_back(
        sides_of((1,), (-1,), (4,), (-4,)), *rest, grad_query, 1000
    )
    four_right, four_left = rotated(four_right, 4), rotated(four_left, -4)
    right, left = kernel_call(
        functools.partial(combine_kernel, block_rows),
        [((block_rows, pair_width), bf16)] * 2,
        [right, left, far_right, far_left, mid_right, mid_left],
        flops=10**8,
        name="combine",
    )
    next_right, next_left = rotated(right, 1), rotated(left, -1)
    (own,), grad_query = attend_back([[slots[0]]], *rest, grad_query)
    returned = [own, next_right, next_left, four_right, four_left, last_right, last_left]
    *parts, first_grads = kernel_call(
        functools.partial(project_back_kernel, len(returned), count),
        halves + [((model_width, 2 * pair_width + 128), bf16)],
        [core, inputs, weights, raw, grad_query, merge_grads, unit_sums, first_sums, second_sums]
        + returned,
        scratch=[pltpu.VMEM((model_width, 2 * pair_width), f32), partial],
        smem=1,
        flops=8 * 10**9,
        name="project_back",
    )
    mine, other = sum_over_tp(*parts)
    input_sum = jnp.where(core[0] == 0, jnp.stack([mine, other]), jnp.stack([other, mine])).reshape(square)
    first_parts = scatter_rows(first_grads)
    second_parts, _ = lax.optimization_barrier((second_parts, first_grads))
    second_states = [
        expand_weight, expand_moment, expand_square, reduce_weight.T, reduce_moment.T, reduce_square.T,
    ]
    second_finished = kernel_call(
        finish_second_kernel,
        [(state.shape, f32) for state in second_states],
        [second_parts] + second_states,
        flops=10**8,
        name="finish_second",
    )
    input_grad = grad_first + input_sum.astype(f32)
    first_parts, input_grad = lax.optimization_barrier((first_parts, input_grad))
    states = [
        entry_weight.transpose(1, 0, 2), entry_moment.transpose(1, 0, 2), entry_square.transpose(1, 0, 2),
        merge_weight.T, merge_moment.T, merge_square.T,
        split_bias, split_moment, split_square, width_params, width_moment, width_square,
    ]
    finished = kernel_call(
        finish_first_kernel,
        [(state.shape, f32) for state in states],
        [first_parts] + states,
        flops=10**8,
        name="finish_first",
    )
    return (
        layer_out,
        input_grad,
        *[array.transpose(1, 0, 2) for array in finished[:3]],
        *[array.T for array in finished[3:6]],
        *second_finished[:3],
        *[array.T for array in second_finished[3:]],
        *finished[6:],
    )


def solution(mesh):
    rows = P("seq", None)
    entry = P("seq", None, "tp")
    across = P("tp", "seq")
    along = P("seq", "tp")
    width = P(None, "seq")
    weights = (entry,) * 3 + (across,) * 3 + (along,) * 3 + (across,) * 3 + (across,) * 3 + (width,) * 3
    return jax.shard_map(
        per_device,
        mesh=mesh,
        in_specs=(rows, rows, P(), rows, rows, P("seq")) + weights,
        out_specs=(rows, rows) + weights,
        check_vma=False,
    )
```

```python
import functools
import math

import jax
import jax.numpy as jnp
from jax import lax
from jax.experimental import pallas as pl
from jax.experimental.pallas import tpu as pltpu
from jax.sharding import PartitionSpec as P

DH = 64
HASHES = 32
STEP = 10
LENGTH = 4096
QUERY_TILE = 256
KEY_TILE = 256
ROW_TILE = 256
WIDTH_LANE = 48
COUNT_LANE = 56
PLANES = 8

UNIT_EPS = 1e-06
NORM_EPS = 1e-05
BETA = 0.5
MATRIX_RATE = 0.02
VECTOR_RATE = 0.5
DECAY = 0.01
ADAM_EPS = 1e-08

f32 = jnp.float32
bf16 = jnp.bfloat16
i32 = jnp.int32


def dot_nt(a, b):
    return lax.dot_general(a, b, (((1,), (1,)), ((), ())), preferred_element_type=f32)


def dot_nn(a, b):
    return lax.dot_general(a, b, (((1,), (0,)), ((), ())), preferred_element_type=f32)


def dot_tn(a, b):
    return lax.dot_general(a, b, (((0,), (0,)), ((), ())), preferred_element_type=f32)


def kernel_call(kernel, outs, operands, scratch=(), smem=0, flops=10**9, name=None, vmem=24):
    spaces = [pltpu.SMEM] * smem + [pltpu.VMEM] * (len(operands) - smem)
    return pl.pallas_call(
        kernel,
        out_shape=[jax.ShapeDtypeStruct(shape, kind) for shape, kind in outs],
        in_specs=[pl.BlockSpec(memory_space=space) for space in spaces],
        out_specs=[pl.BlockSpec(memory_space=pltpu.VMEM)] * len(outs),
        scratch_shapes=list(scratch),
        compiler_params=pltpu.CompilerParams(vmem_limit_bytes=vmem * 2**20),
        cost_estimate=pl.CostEstimate(
            flops=flops,
            bytes_accessed=sum(o.size * o.dtype.itemsize for o in operands),
            transcendentals=0,
        ),
        name=name,
    )(*operands)


def row_tiles(total):
    return [slice(r, r + ROW_TILE) for r in range(0, total, ROW_TILE)]


def left_half(rows):
    return lax.broadcasted_iota(i32, (rows, 2 * DH), 1) < DH


def half_sum(values, mask):
    return jnp.sum(jnp.where(mask, values, 0.0), axis=-1, keepdims=True)


def endings_of(len_ref):
    out = []
    total = jnp.int32(0)
    for s in range(len_ref.shape[0]):
        total = total + len_ref[s]
        out.append(total)
    return out


def labels_of(positions, ends):
    total = jnp.zeros(positions.shape, i32)
    for end in ends:
        total = total + (positions >= end).astype(i32)
    return total


def reach_of(first, last, ends):
    begin = jnp.int32(0)
    finish = jnp.int32(0)
    previous = jnp.int32(0)
    for end in ends:
        begin = jnp.where((first >= previous) & (first < end), previous, begin)
        finish = jnp.where((last >= previous) & (last < end), end, finish)
        previous = end
    return begin, finish


def pair_matches(wide, lane_planes, row_labels, lane_labels):
    parts = []
    for part in range(lane_planes.shape[1] // 128):
        lanes = slice(part * 128, part * 128 + 128)
        same = wide[0] ^ lane_planes[0:1, lanes]
        for b in range(1, PLANES):
            same = same & (wide[b] ^ lane_planes[b : b + 1, lanes])
        parts.append(same)
    matches = lax.population_count(jnp.concatenate(parts, axis=1))
    return jnp.where(row_labels == lane_labels, matches, 0).astype(f32)


def planes_of(codes):
    place = lax.broadcasted_iota(i32, codes.shape, 0)
    rows = []
    for b in range(PLANES):
        bits = ((codes >> b) & 1) << place
        part = bits[0:8] | bits[8:16] | bits[16:24] | bits[24:32]
        part = part | pltpu.roll(part, 4, 0)
        part = part | pltpu.roll(part, 2, 0)
        part = part | pltpu.roll(part, 1, 0)
        rows.append(part[0:1])
    return jnp.concatenate(rows, axis=0)


def block_planes(payload, rows, planes):
    width = payload.shape[1]
    for first in range(0, rows, width):
        place = rows + first // width * HASHES
        codes = payload[place : place + HASHES, :].astype(f32).astype(i32)
        size = min(width, rows - first)
        planes[:, first : first + size] = ~planes_of(codes[:, :size])


def placed(arrays):
    unique = []
    for array, _ in arrays:
        if not any(array is other for other in unique):
            unique.append(array)
    return unique, tuple(([array is other for other in unique].index(True), row) for array, row in arrays)


def attend_kernel(slots, places, len_ref, here_ref, query, own_planes, *refs):
    count = len(slots)
    arrays = 1 + max(index for index, _ in places)
    payloads = [refs[index].at[pl.ds(row, refs[index].shape[0] - row)] for index, row in places]
    refs = refs[arrays:]
    before = None
    if len(refs) == 4 + count:
        before, refs = refs[0], refs[1:]
    out, wide, total, planes = refs[0], refs[1], refs[2], refs[3:]
    block_rows, width = query.shape
    heads = width // 128
    ends = endings_of(len_ref)
    here = here_ref[0] * block_rows
    for (_, _, sent), payload, plane in zip(slots, payloads, planes):
        block_planes(payload, sent, plane)

    def own_tile(own, carry):
        rows = pl.ds(pl.multiple_of(own * QUERY_TILE, QUERY_TILE), QUERY_TILE)
        for b in range(PLANES):
            wide[b] = jnp.broadcast_to(own_planes[rows, b : b + 1], (QUERY_TILE, 128))
        total[...] = jnp.zeros_like(total)
        first = here + own * QUERY_TILE
        begin, finish = reach_of(first, first + (QUERY_TILE - 1), ends)
        row_labels = labels_of(first + lax.broadcasted_iota(i32, (QUERY_TILE, 1), 0), ends)
        for (offset, skipped, sent), keyval, plane in zip(slots, payloads, planes):
            start = here + offset * block_rows + skipped

            @pl.when((begin < start + sent) & (finish > start))
            def _(start=start, sent=sent, keyval=keyval, plane=plane):
                lane_labels = labels_of(start + lax.broadcasted_iota(i32, (1, sent), 1), ends)
                matches = pair_matches(wide, plane[...], row_labels, lane_labels)
                for h in range(heads):
                    lanes = slice(h * 128, h * 128 + 128)
                    pairs = keyval[:sent, lanes]
                    base = dot_nt(query[rows, lanes], pairs) + 1.0
                    base = base * base
                    base = base * base
                    total[:, lanes] += dot_nn((matches * (base * base)).astype(bf16), pairs)

        result = total[...] * (1.0 / (HASHES * 256.0))
        out[rows, :] = result if before is None else before[rows, :] + result
        return carry

    lax.fori_loop(0, block_rows // QUERY_TILE, own_tile, 0)


def back_kernel(slots, places, bundles, len_ref, here_ref, query, upstream, own_planes, *refs):
    count = len(slots)
    arrays = 1 + max(index for index, _ in places)
    payloads = [refs[index].at[pl.ds(row, refs[index].shape[0] - row)] for index, row in places]
    refs = refs[arrays:]
    before = None
    made = len(bundles)
    if len(refs) == 3 + made + count + 1:
        before, refs = refs[0], refs[1:]
    bundled, query_out, wide, total = refs[:made], refs[made], refs[made + 1], refs[made + 2]
    planes = refs[made + 3 :]
    outs = []
    for bundle, out in zip(bundles, bundled):
        filled = 0
        for sent in bundle:
            outs.append(out.at[pl.ds(filled, sent)])
            filled += sent
    block_rows, width = query.shape
    heads = width // 128
    ends = endings_of(len_ref)
    here = here_ref[0] * block_rows
    tiles = block_rows // QUERY_TILE
    query_out[...] = jnp.zeros_like(query_out) if before is None else before[...]
    for (_, _, sent), payload, plane in zip(slots, payloads, planes):
        block_planes(payload, sent, plane)
    for (offset, skipped, sent), keyval, plane, out in zip(slots, payloads, planes, outs):
        start = here + offset * block_rows + skipped
        begin, finish = reach_of(start, start + (sent - 1), ends)
        low = jnp.clip((begin - here) // QUERY_TILE, 0, tiles)
        high = jnp.clip((finish - here + (QUERY_TILE - 1)) // QUERY_TILE, 0, tiles)
        rows = slice(0, sent)
        total[:, rows, :] = jnp.zeros((2, sent, width), f32)

        @pl.when(low < high)
        def _(start=start, sent=sent, rows=rows, low=low, high=high, keyval=keyval, plane=plane):
            columns = jnp.transpose(plane[...])
            for b in range(PLANES):
                wide[b, rows] = jnp.broadcast_to(columns[:, b : b + 1], (sent, 128))
            row_labels = labels_of(start + lax.broadcasted_iota(i32, (sent, 1), 0), ends)

            def add_tile(tile, carry):
                place = pl.ds(pl.multiple_of(tile * QUERY_TILE, QUERY_TILE), QUERY_TILE)
                lane_labels = labels_of(
                    here + tile * QUERY_TILE + lax.broadcasted_iota(i32, (1, QUERY_TILE), 1), ends
                )
                matches = pair_matches(wide[:, rows], own_planes[:, place], row_labels, lane_labels)
                for h in range(heads):
                    lanes = slice(h * 128, h * 128 + 128)
                    pairs = keyval[rows, lanes]
                    asking = query[place, lanes]
                    arriving = upstream[place, lanes]
                    base = dot_nt(pairs, asking) + 1.0
                    grad = dot_nt(pairs, arriving)
                    square = base * base
                    power = matches * ((square * square) * (square * base))
                    grad_low = (grad * power).astype(bf16)
                    total[0, rows, lanes] += dot_nn(grad_low, asking)
                    total[1, rows, lanes] += dot_nn((power * base).astype(bf16), arriving)
                    query_out[place, lanes] += dot_tn(grad_low, pairs) * (4.0 / (HASHES * 128.0))
                return carry

            lax.fori_loop(low, high, add_tile, 0)

        out[...] = (
            total[0, rows] * (4.0 / (HASHES * 128.0)) + total[1, rows] * (1.0 / (HASHES * 256.0))
        ).astype(out.dtype)


def attend(slots, lengths, here, query, own_planes, payloads, before, weight=40000):
    block_rows, width = query.shape
    arrays, places = placed(payloads)
    operands = [lengths, here, query, own_planes, *arrays]
    if before is not None:
        operands.append(before)
    return kernel_call(
        functools.partial(attend_kernel, slots, places),
        [((block_rows, width), f32)],
        operands,
        scratch=[pltpu.VMEM((PLANES, QUERY_TILE, 128), i32), pltpu.VMEM((QUERY_TILE, width), f32)]
        + [pltpu.VMEM((PLANES, sent), i32) for _, _, sent in slots],
        smem=2,
        flops=sum(sent for _, _, sent in slots) * block_rows * weight,
        name="attend",
    )[0]


def attend_back(sides, lengths, here, query, upstream, own_planes, near, before, weight=40000):
    block_rows, width = query.shape
    slots = tuple(slot for side in sides for slot in side)
    bundles = tuple(tuple(sent for _, _, sent in side) for side in sides)
    arrays, places = placed([near[offset] for offset, _, _ in slots])
    operands = [lengths, here, query, upstream, own_planes, *arrays]
    if before is not None:
        operands.append(before)
    *parts, total = kernel_call(
        functools.partial(back_kernel, slots, places, bundles),
        [((sum(bundle), width), bf16) for bundle in bundles] + [((block_rows, width), f32)],
        operands,
        scratch=[pltpu.VMEM((PLANES, block_rows, 128), i32), pltpu.VMEM((2, block_rows, width), f32)]
        + [pltpu.VMEM((PLANES, sent), i32) for _, _, sent in slots],
        smem=2,
        flops=sum(sent for _, _, sent in slots) * block_rows * weight,
        name="attend_back",
    )
    return parts, total


def combine_kernel(block_rows, right, left, far_right, far_left, mid_right, mid_left, to_right, to_left):
    first, second = slice(0, block_rows), slice(block_rows, 2 * block_rows)
    for own, far, across, mid, out in (
        (right, far_right, far_left, mid_right, to_right),
        (left, far_left, far_right, mid_left, to_left),
    ):
        total = own[...].astype(f32) + far[first, :].astype(f32)
        total = total + (across[second, :].astype(f32) + mid[...].astype(f32))
        out[...] = total.astype(bf16)


def unpack(parts, heads, share, entry_bias, expand_bias, vectors, scale, masked):
    ranks, rows, width = parts.shape
    extras = [parts[rank, :, width - 128 :].astype(f32) for rank in range(ranks)]
    firsts = jnp.concatenate([extra[0:1, :] for extra in extras], axis=0).astype(bf16)
    total = ranks * share
    units = total - 3 * DH
    for h in range(heads):
        lane = lax.broadcasted_iota(i32, (128, total), 0)
        place = lax.broadcasted_iota(i32, (128, total), 1)
        moved = (lane == h * share + place % share).astype(f32).astype(bf16)
        spread = dot_nn(firsts, moved)
        owner = lax.broadcasted_iota(i32, (ranks, total), 0)
        at = lax.broadcasted_iota(i32, (ranks, total), 1)
        owned = (at >= owner * share) & (at < owner * share + share)
        biases = jnp.sum(jnp.where(owned, spread, 0.0), axis=0, keepdims=True)
        zeros = jnp.zeros((1, DH), f32)
        half = heads * 2 * DH
        entry_bias[:, h * 2 * DH : h * 2 * DH + 2 * DH] = biases[:, DH : 3 * DH]
        entry_bias[:, half + h * 2 * DH : half + h * 2 * DH + 2 * DH] = jnp.concatenate(
            [biases[:, :DH], zeros], axis=1
        )
        expand_bias[:, h * units : h * units + units] = biases[:, 3 * DH :]
    place = lax.broadcasted_iota(i32, (8, 128), 1) == lax.broadcasted_iota(i32, (8, 128), 0) + WIDTH_LANE
    vectors[...] = dot_nt(
        place.astype(f32).astype(bf16), jnp.concatenate(extras, axis=0).astype(bf16)
    )
    lane = lax.broadcasted_iota(i32, (ranks, 128), 1)
    counts = firsts.astype(f32)
    marked = jnp.where(lane == COUNT_LANE, 256.0 * counts, jnp.where(lane == COUNT_LANE + 1, counts, 0.0))
    marked = jnp.sum(jnp.sum(marked, axis=1, keepdims=True), axis=0, keepdims=True)
    tokens = masked.shape[0] * ranks
    scale[...] = masked[...].astype(f32) * jnp.sqrt(tokens / (marked + 1.0))


def project_kernel(
    heads, share, inputs, parts, query_codes, key_codes, masked,
    raw, query, payload, head, tail, lanes, columns, expand_bias, vectors, scale, weights_out, bias,
):
    unpack(parts, heads, share, bias, expand_bias, vectors, scale, masked)
    shard = parts.shape[1]
    for rank in range(0, parts.shape[0], 2):
        both = jnp.concatenate([parts[rank].astype(f32), parts[rank + 1].astype(f32)], axis=0)
        weights_out[rank * shard : (rank + 2) * shard, :] = both.astype(bf16)
    weights = weights_out
    block_rows = inputs.shape[0]
    width = query.shape[1]
    heads = width // 128
    edge = head.shape[0] - HASHES
    left = left_half(ROW_TILE)
    for rows in row_tiles(block_rows):
        values = dot_nn(inputs[rows, :], weights[:, : 2 * width]) + bias[...]
        raw[rows, :] = values
        for h in range(heads):
            pair = values[:, h * 128 : h * 128 + 128]
            inverse = lax.rsqrt(half_sum(pair * pair, left) + UNIT_EPS)
            payload[rows, h * 128 : h * 128 + 128] = jnp.where(left, pair * inverse, pair).astype(bf16)
            asking = values[:, width + h * 128 : width + h * 128 + 128]
            inverse = lax.rsqrt(half_sum(asking * asking, left) + UNIT_EPS)
            query[rows, h * 128 : h * 128 + 128] = jnp.where(left, asking * inverse, 0.0).astype(bf16)
    codes = key_codes[...].astype(f32).astype(bf16)
    for first in range(0, block_rows, width):
        place = block_rows + first // width * HASHES
        payload[place : place + HASHES, :] = codes[:, first : first + width]
    head[0:edge, :] = payload[0:edge, :]
    tail[0:edge, :] = payload[block_rows - edge : block_rows, :]
    rest = jnp.zeros((HASHES, width - edge), bf16)
    head[edge:, :] = jnp.concatenate([codes[:, :edge], rest], axis=1)
    tail[edge:, :] = jnp.concatenate([codes[:, block_rows - edge :], rest], axis=1)
    planes = planes_of(query_codes[...])
    lanes[...] = planes
    for rows in row_tiles(block_rows):
        columns[rows, :] = jnp.transpose(planes[:, rows])


def halve(core_ref, whole, mine, theirs):
    half = mine.shape[0]
    first = pl.multiple_of(core_ref[0] * half, half)
    mine[...] = whole[pl.ds(first, half), :]
    theirs[...] = whole[pl.ds(half - first, half), :].astype(bf16)


def unite(core_ref, mine, other, whole):
    half = mine.shape[0]
    first = pl.multiple_of(core_ref[0] * half, half)
    whole[pl.ds(first, half), :] = mine[...]
    whole[pl.ds(half - first, half), :] = other[...]


def mix_kernel(core, summed, weights, mixed, mine, theirs, part):
    width = summed.shape[1]
    right = ~left_half(ROW_TILE)
    for rows in row_tiles(summed.shape[0]):
        for h in range(width // 128):
            lanes = slice(h * 128, h * 128 + 128)
            values = summed[rows, lanes]
            inverse = lax.rsqrt(half_sum(values * values, right) * (1.0 / DH) + NORM_EPS)
            mixed[rows, lanes] = jnp.where(right, values * inverse, 0.0).astype(bf16)
        part[rows, :] = dot_nt(mixed[rows, :], weights[:, width : 2 * width])
    halve(core, part, mine, theirs)


def row_mean(values):
    return jnp.sum(values, axis=-1, keepdims=True) * (1.0 / values.shape[-1])


def feed_kernel(
    core, inputs, total, other, vectors, weights, bias, hidden, normed, inverse, active, slope, mine, theirs, attended, part
):
    units = bias.shape[1]
    unite(core, total, other, attended)
    for rows in row_tiles(inputs.shape[0]):
        values = inputs[rows, :].astype(f32) + (attended[rows, :].astype(f32) + vectors[0:1, :])
        centre = values - row_mean(values)
        scale = lax.rsqrt(row_mean(centre * centre) + NORM_EPS)
        unit = centre * scale
        result = unit * vectors[2:3, :] + vectors[3:4, :]
        normed[rows, :] = unit.astype(bf16)
        inverse[rows, :] = scale
        hidden[rows, :] = result.astype(bf16)
        upper = dot_nn(result.astype(bf16), weights[:, :units]) + bias[...]
        curve = 0.5 * (1.0 + lax.erf(upper * math.sqrt(0.5)))
        active[rows, :] = (upper * curve).astype(bf16)
        slope[rows, :] = (
            curve + upper * (jnp.exp(-0.5 * upper * upper) * (1.0 / math.sqrt(2.0 * math.pi)))
        ).astype(bf16)
        part[rows, :] = dot_nt(active[rows, :], weights[:, units:])
    halve(core, part, mine, theirs)


def feed_back_kernel(
    core, hidden, fed_mine, fed_other, cotangent, scale, vectors, weights, active, slope,
    out, second, mine, theirs, grads, width_sums, unit_sums, total, fed, part,
):
    units = active.shape[1]
    unite(core, fed_mine, fed_other, fed)
    total[...] = jnp.zeros_like(total)
    sums = [0.0, 0.0, 0.0]
    unit_sum = 0.0
    for rows in row_tiles(hidden.shape[0]):
        low = hidden[rows, :]
        values = low.astype(f32) + (fed[rows, :].astype(f32) + vectors[1:2, :])
        centre = values - row_mean(values)
        inverse = lax.rsqrt(row_mean(centre * centre) + NORM_EPS)
        normed = centre * inverse
        out[rows, :] = (normed * vectors[4:5, :] + vectors[5:6, :]).astype(bf16)
        upstream = cotangent[rows, :].astype(f32) * scale[rows, :]
        sums[1] += jnp.sum(upstream * normed, axis=0, keepdims=True)
        sums[2] += jnp.sum(upstream, axis=0, keepdims=True)
        scaled = upstream * vectors[4:5, :]
        grad = inverse * (scaled - row_mean(scaled) - normed * row_mean(scaled * normed))
        second[rows, :] = grad
        grad_low = grad.astype(bf16)
        sums[0] += jnp.sum(grad_low.astype(f32), axis=0, keepdims=True)
        upper = (dot_nn(grad_low, weights[:, units:]) * slope[rows, :].astype(f32)).astype(bf16)
        unit_sum += jnp.sum(upper.astype(f32), axis=0, keepdims=True)
        part[rows, :] = dot_nt(upper, weights[:, :units])
        total[:, :units] += dot_tn(low, upper)
        total[:, units:] += dot_tn(grad_low, active[rows, :])
    halve(core, part, mine, theirs)
    grads[...] = total[...].astype(bf16)
    width_sums[...] = jnp.concatenate(sums, axis=0)
    unit_sums[...] = unit_sum


def mix_back_kernel(core, second, came_mine, came_other, normed, inverse, vectors, weights, mixed, summed, first, upstream, grads, width_sums, total, came):
    width = summed.shape[1]
    unite(core, came_mine, came_other, came)
    right = ~left_half(ROW_TILE)
    total[...] = jnp.zeros_like(total)
    sums = [0.0, 0.0, 0.0]
    for rows in row_tiles(second.shape[0]):
        hidden = second[rows, :] + came[rows, :].astype(f32)
        unit = normed[rows, :].astype(f32)
        sums[1] += jnp.sum(hidden * unit, axis=0, keepdims=True)
        sums[2] += jnp.sum(hidden, axis=0, keepdims=True)
        scaled = hidden * vectors[2:3, :]
        grad = inverse[rows, :] * (scaled - row_mean(scaled) - unit * row_mean(scaled * unit))
        first[rows, :] = grad
        grad_low = grad.astype(bf16)
        sums[0] += jnp.sum(grad_low.astype(f32), axis=0, keepdims=True)
        total[...] += dot_tn(grad_low, mixed[rows, :])
        arriving = dot_nn(grad_low, weights[:, width : 2 * width])
        for h in range(width // 128):
            lanes = slice(h * 128, h * 128 + 128)
            values = summed[rows, lanes]
            scale = lax.rsqrt(half_sum(values * values, right) * (1.0 / DH) + NORM_EPS)
            unit = values * scale
            piece = arriving[:, lanes]
            mean = half_sum(piece * unit, right) * (1.0 / DH)
            upstream[rows, lanes] = jnp.where(right, scale * (piece - unit * mean), 0.0).astype(bf16)
    grads[...] = total[...].astype(bf16)
    width_sums[...] = jnp.concatenate(sums, axis=0)


def project_back_kernel(count, ranks, core, inputs, weights, raw, query_grad, merge_grads, unit_sums, first_sums, second_sums, *refs):
    parts, (mine, theirs, grads, total, part) = refs[:count], refs[count:]
    block_rows, width = query_grad.shape
    left = left_half(ROW_TILE)
    total[...] = jnp.zeros_like(total)
    column_sum = 0.0
    for rows in row_tiles(block_rows):
        pieces = []
        for h in range(width // 128):
            lanes = slice(h * 128, h * 128 + 128)
            came = 0.0
            for ref in parts:
                if ref.shape[0] == block_rows:
                    came = came + ref[rows, lanes].astype(f32)
            if rows.start == 0:
                came = came + parts[-2][:, lanes].astype(f32)
            if rows.stop == block_rows:
                came = came + parts[-1][:, lanes].astype(f32)
            values = raw[rows, lanes]
            scale = lax.rsqrt(half_sum(values * values, left) + UNIT_EPS)
            unit = values * scale
            along = half_sum(came * unit, left)
            pieces.append(jnp.where(left, scale * (came - unit * along), came).astype(bf16))
        for h in range(width // 128):
            lanes = slice(h * 128, h * 128 + 128)
            values = raw[rows, width + h * 128 : width + h * 128 + 128]
            scale = lax.rsqrt(half_sum(values * values, left) + UNIT_EPS)
            unit = values * scale
            came = query_grad[rows, lanes]
            along = half_sum(came * unit, left)
            pieces.append(jnp.where(left, scale * (came - unit * along), 0.0).astype(bf16))
        projected = jnp.concatenate(pieces, axis=1)
        column_sum += jnp.sum(projected.astype(f32), axis=0, keepdims=True)
        part[rows, :] = dot_nt(projected, weights[:, : 2 * width])
        total[...] += dot_tn(inputs[rows, :], projected)
    grads[:, :width] = total[:, :width].astype(bf16)
    grads[:, width : 2 * width] = (total[:, width:] + merge_grads[...].astype(f32)).astype(bf16)
    halve(core, part, mine, theirs)
    model_width = grads.shape[0]
    heads = width // (2 * DH)
    units = unit_sums.shape[1] // heads
    share = (3 * DH + units) // ranks
    spread = 0.0
    sources = [(column_sum, width + 2 * DH * h, 0, h, DH) for h in range(heads)]
    sources += [(column_sum, 2 * DH * h, DH, h, 2 * DH) for h in range(heads)]
    sources += [(unit_sums[...], units * h, 3 * DH, h, units) for h in range(heads)]
    for values, first, place, h, size in sources:
        size = size if size > DH else 2 * DH
        row = values[:, first : first + size]
        at = place + lax.broadcasted_iota(i32, (1, size), 1)
        if place == 0:
            row = jnp.where(at < DH, row, 0.0)
        owner = lax.broadcasted_iota(i32, (ranks, size), 0)
        picked = jnp.where((at >= owner * share) & (at < owner * share + share), row, 0.0)
        lane = lax.broadcasted_iota(i32, (size, 128), 1)
        source = place + lax.broadcasted_iota(i32, (size, 128), 0)
        moved = (lane - h * share == source % share) & (lane >= h * share) & (lane < h * share + share)
        spread = spread + dot_nn(picked.astype(bf16), moved.astype(f32).astype(bf16))
    rank_row = lax.broadcasted_iota(i32, (model_width, ranks), 0)
    rank = lax.broadcasted_iota(i32, (model_width, ranks), 1)
    where_to = (rank_row == rank * (model_width // ranks)).astype(f32).astype(bf16)
    width_sums = jnp.concatenate(
        [
            first_sums[0:1, :],
            second_sums[0:1, :],
            first_sums[1:3, :],
            second_sums[1:3, :],
            jnp.zeros((2, model_width), f32),
        ],
        axis=0,
    )
    lane = lax.broadcasted_iota(i32, (8, 128), 1)
    vector = lax.broadcasted_iota(i32, (8, 128), 0)
    vector_lane = ((lane == vector + WIDTH_LANE) & (vector < 6)).astype(f32).astype(bf16)
    grads[:, 2 * width :] = (
        dot_nn(where_to, spread.astype(bf16)) + dot_tn(width_sums.astype(bf16), vector_lane)
    ).astype(bf16)


def unpair(both):
    width = both.shape[1]
    first = [both[:, w : w + DH] for w in range(0, width, 2 * DH)]
    second = [both[:, w + DH : w + 2 * DH] for w in range(0, width, 2 * DH)]
    return jnp.concatenate(first, axis=1), jnp.concatenate(second, axis=1)


def update(grad, state, outs, rate, place=Ellipsis):
    weight, moment, square = (ref[place] for ref in state)
    moment_new = BETA * moment + (1.0 - BETA) * grad
    square_new = BETA * square + (1.0 - BETA) * grad * grad
    fix = 1.0 - BETA**STEP
    outs[0][place] = weight - rate * (
        moment_new * (1.0 / fix) / (jnp.sqrt(square_new * (1.0 / fix)) + ADAM_EPS) + DECAY * weight
    )
    outs[1][place] = moment_new
    outs[2][place] = square_new


def sum_of(parts):
    total = parts[0].astype(f32)
    for index in range(1, parts.shape[0]):
        total = total + parts[index].astype(f32)
    return total


def finish_first_kernel(parts, *refs):
    state, outs = refs[:12], refs[12:]
    total = sum_of(parts)
    width = state[3].shape[1]
    key, value = unpair(total[:, : 2 * width])
    query, merge = unpair(total[:, 2 * width : 4 * width])
    for which, grad in enumerate((query, key, value)):
        update(grad, state[0:3], outs[0:3], MATRIX_RATE, which)
    update(merge, state[3:6], outs[3:6], MATRIX_RATE)
    rest = total[:, 4 * width :]
    size = state[6].shape[1]
    for row in range(state[6].shape[0]):
        update(rest[0:1, row * size : row * size + size], state[6:9], outs[6:9], VECTOR_RATE, (slice(row, row + 1), slice(None)))
    update(jnp.transpose(rest)[WIDTH_LANE : WIDTH_LANE + 6, :], state[9:12], outs[9:12], VECTOR_RATE)


def finish_second_kernel(parts, *refs):
    state, outs = refs[:6], refs[6:]
    total = sum_of(parts)
    units = state[0].shape[1]
    update(total[:, :units], state[0:3], outs[0:3], MATRIX_RATE)
    update(total[:, units:], state[3:6], outs[3:6], MATRIX_RATE)


def pack_kernel(entry, merge, width, split, masked, expand, reduce, out, later):
    rows = entry.shape[1]
    pieces = []
    for first, second in ((entry[1], entry[2]), (entry[0], merge[...])):
        for h in range(0, entry.shape[2], DH):
            pieces += [first[:, h : h + DH], second[:, h : h + DH]]
    heads, size = split.shape
    lane = lax.broadcasted_iota(i32, (size, 128), 1)
    index = lax.broadcasted_iota(i32, (size, 128), 0)
    biases = 0.0
    for h in range(heads):
        moved = (lane == index + h * size).astype(f32).astype(bf16)
        biases = biases + dot_nn(split[h : h + 1, :].astype(bf16), moved)
    marked = jnp.sum(jnp.sum(masked[...].astype(f32), axis=1, keepdims=True), axis=0, keepdims=True)
    high = jnp.floor(marked * (1.0 / 256.0))
    lane = lax.broadcasted_iota(i32, (1, 128), 1)
    biases = biases + jnp.where(lane == COUNT_LANE, high, 0.0)
    biases = biases + jnp.where(lane == COUNT_LANE + 1, marked - 256.0 * high, 0.0)
    place = (
        lax.broadcasted_iota(i32, (6, 128), 1) == lax.broadcasted_iota(i32, (6, 128), 0) + WIDTH_LANE
    )
    vectors = dot_tn(width[...].astype(bf16), place.astype(f32).astype(bf16))
    first_row = lax.broadcasted_iota(i32, (rows, 128), 0) == 0
    pieces.append(vectors + jnp.where(first_row, biases, 0.0))
    packed = jnp.concatenate(pieces, axis=1).astype(bf16)
    rest = jnp.concatenate([expand[...].astype(bf16), reduce[...].astype(bf16)], axis=1)
    for rank in range(out.shape[0]):
        out[rank] = packed
        later[rank] = rest


def shifted(value, steps):
    count = lax.axis_size("seq")
    return lax.ppermute(
        value, "seq", [(i, i + steps) for i in range(count) if 0 <= i + steps < count]
    )


def rotated(value, steps):
    count = lax.axis_size("seq")
    return lax.ppermute(value, "seq", [(i, (i + steps) % count) for i in range(count)])


def scatter_rows(grads):
    count = lax.axis_size("seq")
    sent = grads.astype(bf16).reshape((count, grads.shape[0] // count) + grads.shape[1:])
    return lax.all_to_all(sent, "seq", 0, 0, tiled=True)


def swapped(value, mask):
    return lax.ppermute(value, "tp", [(i, i ^ mask) for i in range(lax.axis_size("tp"))])


def sum_over_tp(mine, theirs):
    here = (mine + swapped(theirs, 1).astype(f32)).astype(bf16)
    there = swapped(here, 2)
    total = (here.astype(f32) + there.astype(f32)).astype(bf16)
    return total, swapped(total, 1)


def per_device(
    inputs,
    cotangent,
    lengths,
    query_codes,
    key_codes,
    masked,
    entry_weight,
    entry_moment,
    entry_square,
    merge_weight,
    merge_moment,
    merge_square,
    expand_weight,
    expand_moment,
    expand_square,
    reduce_weight,
    reduce_moment,
    reduce_square,
    split_bias,
    split_moment,
    split_square,
    width_params,
    width_moment,
    width_square,
):
    block_rows, model_width = inputs.shape
    count = lax.axis_size("seq")
    total_tokens = block_rows * count
    reach = (LENGTH - 2) // block_rows + 1
    heads = split_bias.shape[0]
    local = heads * DH
    shard_rows = model_width // count
    hidden_units = expand_weight.shape[1]
    split_columns = split_bias.shape[1]
    here_index = lax.axis_index("seq")
    here = here_index.astype(i32).reshape(1)

    extra = 4 * local
    first_shards, second_shards = kernel_call(
        pack_kernel,
        [((count, shard_rows, extra + 128), bf16), ((count, shard_rows, 2 * hidden_units), bf16)],
        [
            entry_weight.transpose(1, 0, 2), merge_weight.T, width_params, split_bias,
            masked.reshape(-1, 128), expand_weight, reduce_weight.T,
        ],
        flops=10**8,
        name="pack",
    )
    first_full = lax.all_to_all(first_shards, "seq", 0, 0, tiled=True)
    far = KEY_TILE * -(-(LENGTH - 1 - (reach - 1) * block_rows) // KEY_TILE)
    slots = {0: (0, 0, block_rows)}
    for distance in range(1, reach):
        slots[distance] = (distance, 0, block_rows)
        slots[-distance] = (-distance, 0, block_rows)
    slots[reach] = (reach, 0, far)
    slots[-reach] = (-reach, block_rows - far, far)

    pair_width = 2 * local
    code_rows = HASHES * -(-block_rows // pair_width)
    (
        raw, query, whole, head, tail, query_lanes, query_columns, expand_bias, vectors, scale, weights
    ) = kernel_call(
        functools.partial(project_kernel, heads, split_columns),
        [
            ((block_rows, 2 * pair_width), f32),
            ((block_rows, pair_width), bf16),
            ((block_rows + code_rows, pair_width), bf16),
            ((far + HASHES, pair_width), bf16),
            ((far + HASHES, pair_width), bf16),
            ((PLANES, block_rows), i32),
            ((block_rows, PLANES), i32),
            ((1, hidden_units), f32),
            ((8, model_width), f32),
            ((block_rows, 1), f32),
            ((model_width, extra + 128), bf16),
        ],
        [inputs, first_full, query_codes.T, key_codes.T, masked.reshape(-1, 1)],
        scratch=[pltpu.VMEM((1, 2 * pair_width), f32)],
        flops=10**9,
        name="project",
    )
    near = {0: (whole, 0)}
    for side in (1, -1):
        near[side] = (rotated(whole, -side), 0)
        near[4 * side] = (rotated(whole, -4 * side), 0)
    both = jnp.concatenate([near[1][0], near[-1][0]], axis=0)
    for side in (1, -1):
        near[2 * side] = (rotated(near[side][0], -side), 0)
        got = rotated(both, -4 * side)
        near[4 * side + 1] = (got, 0)
        near[4 * side - 1] = (got, whole.shape[0])
    summed = None
    for offsets in ((0,), (1, -1, 4, -4), (2, -2), (3, 5, -3, -5, reach, -reach)):
        if offsets[0] == 2:
            second_shards, got = lax.optimization_barrier((second_shards, near[2][0]))
            near[2] = (got, 0)
            second_full = lax.all_to_all(second_shards, "seq", 0, 0, tiled=True)
            second_full = second_full.reshape(model_width, -1)
        chosen = tuple(slots[o] for o in offsets)
        summed = attend(
            chosen, lengths, here, query, query_columns, [near[o] for o in offsets], summed,
        )
        if offsets[0] == 1:
            head, tail, summed = lax.optimization_barrier((head, tail, summed))
            near[reach], near[-reach] = (shifted(head, -reach), 0), (shifted(tail, reach), 0)

    summed, second_full = lax.optimization_barrier((summed, second_full))

    square = (block_rows, model_width)
    halves = [((block_rows // 2, model_width), f32), ((block_rows // 2, model_width), bf16)]
    core = (lax.axis_index("tp") % 2).astype(i32).reshape(1)
    united = pltpu.VMEM(square, bf16)
    partial = pltpu.VMEM(square, f32)
    mixed, *parts = kernel_call(
        mix_kernel,
        [((block_rows, pair_width), bf16)] + halves,
        [core, summed, weights],
        scratch=[partial],
        smem=1,
        flops=3 * 10**9,
        name="mix",
    )
    attended = sum_over_tp(*parts)
    hidden, normed, inverse, active, slope, *parts = kernel_call(
        feed_kernel,
        [
            (square, bf16),
            (square, bf16),
            ((block_rows, 1), f32),
            ((block_rows, hidden_units), bf16),
            ((block_rows, hidden_units), bf16),
        ]
        + halves,
        [core, inputs, *attended, vectors, second_full, expand_bias],
        scratch=[united, partial],
        smem=1,
        flops=8 * 10**9,
        name="feed",
    )
    fed = sum_over_tp(*parts)

    layer_out, grad_second, *parts, second_grads, second_sums, unit_sums = kernel_call(
        feed_back_kernel,
        [
            (square, bf16),
            (square, f32),
            *halves,
            ((model_width, 2 * hidden_units), bf16),
            ((3, model_width), f32),
            ((1, hidden_units), f32),
        ],
        [core, hidden, *fed, cotangent, scale, vectors, second_full, active, slope],
        scratch=[pltpu.VMEM((model_width, 2 * hidden_units), f32), united, partial],
        smem=1,
        flops=10 * 10**9,
        name="feed_back",
    )
    came = sum_over_tp(*parts)
    second_parts = scatter_rows(second_grads)
    grad_first, upstream, merge_grads, first_sums = kernel_call(
        mix_back_kernel,
        [
            (square, f32),
            ((block_rows, pair_width), bf16),
            ((model_width, pair_width), bf16),
            ((3, model_width), f32),
        ],
        [core, grad_second, *came, normed, inverse, vectors, weights, mixed, summed],
        scratch=[pltpu.VMEM((model_width, pair_width), f32), united],
        smem=1,
        flops=6 * 10**9,
        name="mix_back",
    )
    def sides_of(*offsets):
        return [[slots[o] for o in side] for side in offsets]

    rest = (lengths, here, query, upstream, query_lanes, near)
    (right, left), grad_query = attend_back(sides_of((5, 3), (-5, -3)), *rest, None)
    far_right, far_left = rotated(right, 4), rotated(left, -4)
    second_parts, grad_query = lax.optimization_barrier((second_parts, grad_query))
    (right, left, last_right, last_left), grad_query = attend_back(
        sides_of((2,), (-2,), (reach,), (-reach,)), *rest, grad_query
    )
    mid_right, mid_left = rotated(right, 1), rotated(left, -1)
    last_right, last_left = rotated(last_right, reach), rotated(last_left, -reach)
    (right, left, four_right, four_left), grad_query = attend_back(
        sides_of((1,), (-1,), (4,), (-4,)), *rest, grad_query, 1000
    )
    four_right, four_left = rotated(four_right, 4), rotated(four_left, -4)
    right, left = kernel_call(
        functools.partial(combine_kernel, block_rows),
        [((block_rows, pair_width), bf16)] * 2,
        [right, left, far_right, far_left, mid_right, mid_left],
        flops=10**8,
        name="combine",
    )
    next_right, next_left = rotated(right, 1), rotated(left, -1)
    (own,), grad_query = attend_back([[slots[0]]], *rest, grad_query)
    returned = [own, next_right, next_left, four_right, four_left, last_right, last_left]
    *parts, first_grads = kernel_call(
        functools.partial(project_back_kernel, len(returned), count),
        halves + [((model_width, 2 * pair_width + 128), bf16)],
        [core, inputs, weights, raw, grad_query, merge_grads, unit_sums, first_sums, second_sums]
        + returned,
        scratch=[pltpu.VMEM((model_width, 2 * pair_width), f32), partial],
        smem=1,
        flops=8 * 10**9,
        name="project_back",
    )
    mine, other = sum_over_tp(*parts)
    input_sum = jnp.where(core[0] == 0, jnp.stack([mine, other]), jnp.stack([other, mine])).reshape(square)
    first_parts = scatter_rows(first_grads)
    second_parts, _ = lax.optimization_barrier((second_parts, first_grads))
    second_states = [
        expand_weight, expand_moment, expand_square, reduce_weight.T, reduce_moment.T, reduce_square.T,
    ]
    second_finished = kernel_call(
        finish_second_kernel,
        [(state.shape, f32) for state in second_states],
        [second_parts] + second_states,
        flops=10**8,
        name="finish_second",
    )
    input_grad = grad_first + input_sum.astype(f32)
    first_parts, input_grad = lax.optimization_barrier((first_parts, input_grad))
    states = [
        entry_weight.transpose(1, 0, 2), entry_moment.transpose(1, 0, 2), entry_square.transpose(1, 0, 2),
        merge_weight.T, merge_moment.T, merge_square.T,
        split_bias, split_moment, split_square, width_params, width_moment, width_square,
    ]
    finished = kernel_call(
        finish_first_kernel,
        [(state.shape, f32) for state in states],
        [first_parts] + states,
        flops=10**8,
        name="finish_first",
    )
    return (
        layer_out,
        input_grad,
        *[array.transpose(1, 0, 2) for array in finished[:3]],
        *[array.T for array in finished[3:6]],
        *second_finished[:3],
        *[array.T for array in second_finished[3:]],
        *finished[6:],
    )


def solution(mesh):
    rows = P("seq", None)
    entry = P("seq", None, "tp")
    across = P("tp", "seq")
    along = P("seq", "tp")
    width = P(None, "seq")
    weights = (entry,) * 3 + (across,) * 3 + (along,) * 3 + (across,) * 3 + (across,) * 3 + (width,) * 3
    return jax.shard_map(
        per_device,
        mesh=mesh,
        in_specs=(rows, rows, P(), rows, rows, P("seq")) + weights,
        out_specs=(rows, rows) + weights,
        check_vma=False,
    )
```
